128 devices in a mesh: parts: 1, seq: 16 (over y, x), head: 8 (over z, core).
Axes of the slice: x: 4, y: 4, z: 4, core: 2. Of those that a mesh axis runs over, the one named last changes fastest.
Arguments:
- prompt_x: bfloat16 [2048, 8192], P(('parts', 'seq'), 'head'), may hold values from -6 to 6
- prompt_b: bfloat16 [2048, 1024], P(('parts', 'seq'), 'head'), may hold values from -0.5 to 0.5
- prompt_dt: float32 [128, 2048], P('head', ('parts', 'seq')), may hold values from 0.5 to 2
- branch_x: bfloat16 [2048, 8192], P(('parts', 'seq'), 'head'), may hold values from -6 to 6
- branch_b: bfloat16 [2048, 1024], P(('parts', 'seq'), 'head'), may hold values from -0.5 to 0.5
- branch_c: bfloat16 [2048, 1024], P(('parts', 'seq'), 'head'), may hold values from -0.5 to 0.5
- branch_z: bfloat16 [2048, 8192], P(('parts', 'seq'), 'head'), may hold values from -6 to 6
- branch_dt: float32 [128, 2048], P('head', ('parts', 'seq')), may hold values from 0.5 to 2
- a_rate: float32 [128], P('head'), may hold values from 0.00024414062 to 0.05
- d_skip: float32 [128], P('head'), may hold values from 0.5 to 1.5
- norm_gain: float32 [8192], P('head'), may hold values from 0.5 to 1.5
- branch_parent: int32 [64], P(('parts', 'seq')), may hold values from 0 to 15
- group_ids: int32 [2048], P(('parts', 'seq')), may hold values from 0 to 7, as said below
- returns: float32 [2048], P(('parts', 'seq')), may hold values from -6 to 6
- out_grad: bfloat16 [2048, 8192], P(('parts', 'seq'), 'head'), may hold values from -6 to 6
Outputs:
- branch_out: bfloat16 [2048, 8192], P(('parts', 'seq'), 'head')
- branch_grad: bfloat16 [2048, 8192], P(('parts', 'seq'), 'head')
- prompt_grad: float32 [2048, 8192], P(('parts', 'seq'), 'head')
The draws below stay inside these ranges and needn't reach their ends.
Inputs may be any that keep to these rules, and one draw needn't show every extreme that they name: `group_ids`: exactly one advantage group other than 0 and 7 holds no token; which one varies.
All inputs are finite; a program needn't handle non-finite values.
Results may differ from the reference program's by a relative error of at most 0.0095.
Values may be sent and summed in bfloat16 or wider, within the bound.
A program may use at most 128 MiB of HBM per device.

```python
import math
import jax
import jax.numpy as jnp
from jax import lax

HEADS = 128
HEAD_DIM = 64
STATE = 128
GROUPS = 8
WIDTH = 8192
BLOCK = 128
SEG = 32
ADV_GROUPS = 8
PROMPT = 2048
NBR = 64
BTOK = 2048


def draw_group_ids(key, part):
    key = jax.random.fold_in(key, 7)
    first_key, second_key = jax.random.split(key)
    empty_group = jax.random.randint(first_key, (), 1, ADV_GROUPS - 1)
    labels = jax.random.randint(second_key, (BTOK,), 0, ADV_GROUPS - 1)
    labels = labels + (labels >= empty_group).astype(jnp.int32)
    positions = jnp.arange(BTOK, dtype=jnp.int32)
    labels = jnp.where(positions == 0, 0, labels)
    labels = jnp.where(positions == 1, ADV_GROUPS - 1, labels)
    return labels.astype(jnp.int32)


def touch_ends(array, rng, least, largest):
    place = [jax.random.randint(jax.random.fold_in(rng, axis), (), 0, length) for axis, length in enumerate(array.shape)]
    main_axis = array.shape.index(max(array.shape))
    next_to = place[:main_axis] + [(place[main_axis] + 1) % array.shape[main_axis]] + place[main_axis + 1:]
    return array.at[tuple(place)].set(least).at[tuple(next_to)].set(largest)


def levels(own_key, shape, shards, low, high):
    loudness, own = 1.0, jax.random.fold_in(own_key, 6)
    for position, shards_of in shards:
        heights = jnp.exp(jax.random.uniform(jax.random.fold_in(own, position), (shards_of,), jnp.float32, low / len(shards), high / len(shards)))
        loudness = loudness * jnp.repeat(heights, shape[position] // shards_of).reshape([-1 if axis == position else 1 for axis in range(len(shape))])
    return loudness


def bell_draw(stream_key, extent, scale, limit, shards=(), kind=jnp.bfloat16):
    drawn = jax.random.normal(stream_key, extent, jnp.float32) * scale
    if len(shards) > 0:
        drawn = levels(stream_key, extent, shards, -0.22, 0.18) * drawn
    return jnp.clip(drawn, min=-limit, max=limit).astype(kind)


def setup_inputs(seed: int = 0, part: int = 0) -> dict:
    key_of = jax.random.split(jax.random.key(seed), 16)
    part_splits = jax.random.split(jax.random.fold_in(key_of[15], part), 16)
    return {
        "prompt_x": bell_draw(part_splits[0], (PROMPT, WIDTH), 1.0, 6.0, ((0, 16), (1, 8))),
        "prompt_b": bell_draw(part_splits[1], (PROMPT, GROUPS * STATE), STATE ** -0.5, 0.5, ((0, 16), (1, 8))),
        "prompt_dt": jnp.clip(jnp.exp(math.log(2.0) - 1.3862944 * jax.random.uniform(part_splits[2], (HEADS, PROMPT), jnp.float32) ** levels(part_splits[2], (HEADS, PROMPT), ((0, 8), (1, 16)), -0.2, 0.2)), 0.5, 2.0),
        "branch_x": bell_draw(part_splits[3], (BTOK, WIDTH), 1.0, 6.0, ((0, 16), (1, 8))),
        "branch_b": bell_draw(part_splits[4], (BTOK, GROUPS * STATE), STATE ** -0.5, 0.5, ((0, 16), (1, 8))),
        "branch_c": bell_draw(part_splits[5], (BTOK, GROUPS * STATE), STATE ** -0.5, 0.5, ((0, 16), (1, 8))),
        "branch_z": bell_draw(part_splits[6], (BTOK, WIDTH), 1.0, 6.0, ((0, 16), (1, 8))),
        "branch_dt": jnp.clip(jnp.exp(math.log(2.0) - 1.3862944 * jax.random.uniform(part_splits[7], (HEADS, BTOK), jnp.float32) ** levels(part_splits[7], (HEADS, BTOK), ((0, 8), (1, 16)), -0.2, 0.2)), 0.5, 2.0),
        "a_rate": jnp.clip(jnp.exp(math.log(0.05) - 5.322034 * jax.random.uniform(key_of[8], (HEADS,), jnp.float32) ** levels(key_of[8], (HEADS,), ((0, 8),), -0.2, 0.2)), 0.00024414062, 0.05),
        "d_skip": jnp.clip(0.5 + 1.0 * jax.random.uniform(key_of[9], (HEADS,), jnp.float32) ** levels(key_of[9], (HEADS,), ((0, 8),), -0.2, 0.2), 0.5, 1.5),
        "norm_gain": jnp.clip(1.0 + 0.1 * jax.random.normal(key_of[10], (WIDTH,), jnp.float32), 0.5, 1.5),
        "branch_parent": touch_ends(jax.random.randint(part_splits[11], (NBR,), 0, PROMPT // BLOCK), jax.random.fold_in(part_splits[11], 1), 0, (PROMPT // BLOCK) - 1).astype(jnp.int32),
        "group_ids": draw_group_ids(jax.random.fold_in(jax.random.fold_in(key_of[15], part), 71), part),
        "returns": bell_draw(part_splits[13], (BTOK,), 1.0, 6.0, ((0, 16),), jnp.float32),
        "out_grad": bell_draw(part_splits[14], (BTOK, WIDTH), 1.0, 6.0, ((0, 16), (1, 8))),
    }


EPSILON = 1e-05
PRECISE = lax.Precision.HIGHEST

def expand_groups(values, repeat_count):
    rows = values.shape[0]
    grouped = values.astype(jnp.float32).reshape(rows, -1, STATE)
    return jnp.repeat(grouped, repeat_count, axis=1)

def block_weights(step_sizes, rates, block):
    heads, length = step_sizes.shape
    logs = (step_sizes * (-rates)[:, None]).reshape(heads, length // block, block)
    running = jnp.cumsum(logs, axis=2)
    totals = running[:, :, -1]
    tails = jnp.exp(totals[:, :, None] - running) * step_sizes.reshape(heads, length // block, block)
    return (tails, totals)

def block_updates(inputs, projections, step_sizes, rates):
    tails, totals = block_weights(step_sizes, rates, BLOCK)
    heads = step_sizes.shape[0]
    count = totals.shape[1]
    values = inputs.astype(jnp.float32).reshape(count, BLOCK, heads, HEAD_DIM)
    loads = expand_groups(projections, HEADS // GROUPS).reshape(count, BLOCK, heads, STATE)
    weighted = values * jnp.transpose(tails, (1, 2, 0))[..., None]
    updates = jnp.einsum('kqhp,kqhn->khpn', weighted, loads, precision=PRECISE)
    return (updates, tails, totals, loads)

def chain_blocks(updates, totals):

    def advance(carry, item):
        update, total = item
        carry = jnp.exp(total)[:, None, None] * carry + update
        return (carry, carry)
    _, ends = lax.scan(advance, jnp.zeros_like(updates[0]), (updates, totals.T))
    return ends

def back_chain(arriving, totals):

    def retreat(carry, item):
        gradient, decay = carry
        incoming, total = item
        gradient = incoming + decay[:, None, None] * gradient
        return ((gradient, jnp.exp(total)), gradient)
    start = (jnp.zeros_like(arriving[0]), jnp.ones_like(totals[:, 0]))
    _, gradients = lax.scan(retreat, start, (arriving, totals.T), reverse=True)
    return gradients

def prompt_gradient(gradients, tails, loads):
    count = gradients.shape[0]
    heads = gradients.shape[1]
    applied = jnp.einsum('khpn,kqhn->kqhp', gradients, loads, precision=PRECISE)
    applied = applied * jnp.transpose(tails, (1, 2, 0))[..., None]
    return applied.reshape(count * BLOCK, heads * HEAD_DIM)

def branch_forward(inputs, in_proj, out_proj, step_sizes, rates, skips, forks):
    rows = inputs.shape[0]
    heads = step_sizes.shape[0]
    branches = rows // SEG
    logs = (step_sizes * (-rates)[:, None]).reshape(heads, branches, SEG)
    running = jnp.cumsum(logs, axis=2)
    values = inputs.astype(jnp.float32).reshape(branches, SEG, heads, HEAD_DIM)
    loads = expand_groups(in_proj, HEADS // GROUPS).reshape(branches, SEG, heads, STATE)
    reads = expand_groups(out_proj, HEADS // GROUPS).reshape(branches, SEG, heads, STATE)
    differ = running[:, :, :, None] - running[:, :, None, :]
    lower = jnp.arange(SEG, dtype=jnp.int32)[:, None] >= jnp.arange(SEG, dtype=jnp.int32)[None, :]
    decays = jnp.where(lower[None, None], jnp.exp(jnp.minimum(differ, 0.0)), 0.0)
    steps_bt = step_sizes.reshape(heads, branches, SEG)
    scores = jnp.einsum('bthn,bshn->bhts', reads, loads, precision=PRECISE)
    mixing = scores * jnp.transpose(decays, (1, 0, 2, 3)) * jnp.transpose(steps_bt, (1, 0, 2))[:, :, None, :]
    inner = jnp.einsum('bhts,bshp->bthp', mixing, values, precision=PRECISE)
    lift = jnp.transpose(jnp.exp(running), (1, 2, 0))
    carried = jnp.einsum('bthn,bhpn->bthp', reads, forks, precision=PRECISE) * lift[..., None]
    output = inner + carried + skips[None, None, :, None] * values
    return (output.reshape(rows, heads * HEAD_DIM), mixing, lift, reads)

def branch_backward(cotangent, mixing, lift, reads, skips):
    branches, heads = (mixing.shape[0], mixing.shape[1])
    upstream = cotangent.reshape(branches, SEG, heads, HEAD_DIM)
    inputs_grad = jnp.einsum('bhts,bthp->bshp', mixing, upstream, precision=PRECISE)
    inputs_grad = inputs_grad + skips[None, None, :, None] * upstream
    state_grads = jnp.einsum('bthn,bthp->bhpn', reads * lift[..., None], upstream, precision=PRECISE)
    return (inputs_grad.reshape(branches * SEG, heads * HEAD_DIM).astype(jnp.bfloat16), state_grads)

def group_table(group_ids):
    return (group_ids[:, None] == jnp.arange(ADV_GROUPS, dtype=jnp.int32)[None, :]).astype(jnp.float32)

def group_terms(group_ids, returns):
    table = group_table(group_ids)
    counts = lax.optimization_barrier(jnp.sum(table, axis=0))
    sums = jnp.dot(returns, table, precision=PRECISE)
    squares = jnp.dot(returns * returns, table, precision=PRECISE)
    return (counts, sums, squares)

def advantages(stats, group_ids, returns):
    counts, sums, squares = stats
    table = group_table(group_ids)
    floor_count = jnp.maximum(counts, 1.0)
    means = sums / floor_count
    spread = jnp.sqrt(squares / floor_count - means * means + 1.0)
    token_mean = jnp.dot(table, means, precision=PRECISE)
    token_spread = jnp.dot(table, spread, precision=PRECISE)
    return (returns - token_mean) / token_spread

def reference(prompt_x, prompt_b, prompt_dt, branch_x, branch_b, branch_c, branch_z, branch_dt, a_rate, d_skip, norm_gain, branch_parent, group_ids, returns, out_grad):
    updates, tails, totals, loads = block_updates(prompt_x, prompt_b, prompt_dt, a_rate)
    ends = chain_blocks(updates, totals)
    chosen = (branch_parent[:, None] == jnp.arange(ends.shape[0], dtype=jnp.int32)[None, :]).astype(jnp.float32)
    forks = jnp.einsum('bm,mhpn->bhpn', chosen, ends, precision=PRECISE)
    output, mixing, lift, reads = branch_forward(branch_x, branch_b, branch_c, branch_dt, a_rate, d_skip, forks)
    opened = jax.nn.silu(branch_z.astype(jnp.float32))
    gated = output * opened
    total_sq = lax.optimization_barrier(jnp.sum(gated * gated, axis=1))
    scale = lax.rsqrt(total_sq / (HEADS * HEAD_DIM) + EPSILON)
    branch_out = (gated * scale[:, None] * norm_gain[None, :]).astype(jnp.bfloat16)
    weights = advantages(group_terms(group_ids, returns), group_ids, returns)
    pushed = out_grad.astype(jnp.float32) * weights[:, None] * norm_gain[None, :]
    along = lax.optimization_barrier(jnp.sum(pushed * gated, axis=1))
    cotangent = (scale[:, None] * pushed - gated * (scale * scale * scale * along / (HEADS * HEAD_DIM))[:, None]) * opened
    branch_grad, state_grads = branch_backward(cotangent, mixing, lift, reads, d_skip)
    arriving = jnp.einsum('bm,bhpn->mhpn', chosen, state_grads, precision=PRECISE)
    gradients = back_chain(arriving, totals)
    prompt_grad = prompt_gradient(gradients, tails, loads)
    return (branch_out, branch_grad, prompt_grad)
```

```python
import functools

import jax
import jax.numpy as jnp
from jax import lax
from jax.experimental import pallas as pl
from jax.experimental.pallas import tpu as pltpu
from jax.sharding import PartitionSpec as P

HEADS = 128
HEAD_DIM = 64
STATE = 128
BLOCK = 128
SEG = 32
NB = 4
EPSILON = 1e-05
SIDE = 4
LOCAL_HEADS = 16
CH = 1024
HALF = 512
NCH = 2
CW = HALF // NCH
MESH_ID = pl.DeviceIdType.MESH
F32 = jnp.float32
BF16 = jnp.bfloat16
HIGH = lax.Precision.HIGHEST


def iota(shape, dim):
    return lax.broadcasted_iota(jnp.int32, shape, dim)


def column(row, n):
    eye = iota((n, n), 0) == iota((n, n), 1)
    return jnp.sum(jnp.where(eye, jnp.broadcast_to(row, (n, n)), 0.0), axis=1, keepdims=True)


def split(v):
    high = v.astype(BF16).astype(F32)
    return high, v - high


def mm(a, b):
    return jnp.dot(a, b, preferred_element_type=F32)


def rows_to_tokens(w, width):
    return jnp.concatenate([jnp.broadcast_to(w[b : b + 1], (SEG, width)) for b in range(NB)], axis=0)


def kernel(
    px, pb, pdt, bx, bb, bc, bz, bdt, rate, skip, gain, par, gid, ret, og,
    out_o, grad_o, prompt_o,
    pk, ar, ug, cg, ct, yp, yr, dg, gp, gr, acc, wt, tail_e, lift_e, einv_e, smat, y_s, gated_s, sz_s, dy_s,
    pk_s, pk_r, ar_s, ar_r, u_s, u_r, c_s, c_r, y_ss, y_rs, d_s, d_r, g_s, g_r,
):
    seq = lax.axis_index("seq")
    head = lax.axis_index("head")
    yi, xi = seq // SIDE, seq % SIDE

    barrier = pltpu.get_barrier_semaphore()
    for r in range(1, 16):
        pl.semaphore_signal(barrier, inc=1, device_id={"seq": (seq + r) % 16}, device_id_type=MESH_ID)
    for r in range(1, 8):
        pl.semaphore_signal(barrier, inc=1, device_id={"head": (head + r) % 8}, device_id_type=MESH_ID)

    first = (xi, yi)
    second = (yi, xi)

    def at(half, f, s):
        return s * SIDE + f if half == 0 else f * SIDE + s

    def send(src, dst, s_sem, r_sem, device):
        copy = pltpu.make_async_remote_copy(
            src_ref=src, dst_ref=dst, send_sem=s_sem, recv_sem=r_sem, device_id=device, device_id_type=MESH_ID
        )
        copy.start()
        return copy

    rate_c = column(rate[...], LOCAL_HEADS)
    upto = (iota((BLOCK, BLOCK), 0) <= iota((BLOCK, BLOCK), 1)).astype(F32)
    same = (iota((BLOCK, BLOCK), 0) // SEG) == (iota((BLOCK, BLOCK), 1) // SEG)
    upto_seg = jnp.where(same, upto, 0.0)
    p_dt = pdt[...]
    running = jnp.dot(p_dt * (-rate_c), upto, precision=HIGH, preferred_element_type=F32)
    total = running[:, BLOCK - 1 :]
    tails = jnp.exp(total - running) * p_dt
    b_dt = bdt[...]
    cum = jnp.dot(b_dt * (-rate_c), upto_seg, precision=HIGH, preferred_element_type=F32)
    lift = jnp.exp(cum)
    einv = jnp.exp(-cum) * b_dt

    stack = jnp.concatenate(
        [*split(tails), *split(lift), *split(einv), jnp.zeros((32, BLOCK), F32)], axis=0
    )
    stack_t = stack.T.astype(BF16)
    spread32 = ((iota((32, CH), 0) & 15) == (iota((32, CH), 1) >> 6)).astype(BF16)
    spread16 = ((iota((16, CH), 0)) == (iota((16, CH), 1) >> 6)).astype(F32)
    te = mm(stack_t[:, 0:32], spread32)
    tail_e[...] = te
    xw = (px[...].astype(F32) * te).astype(BF16)
    pb_t = pb[...].astype(F32).T.astype(BF16)
    for half in range(2):
        for c in range(NCH):
            lo = half * HALF + c * CW
            ug[half, c, first[half]] = mm(pb_t, xw[:, lo : lo + CW]).astype(BF16)

    sub = iota((8, 128), 0)
    lane = iota((8, 128), 1)
    eye16 = iota((16, 128), 0) == iota((16, 128), 1)
    total_row = jnp.sum(jnp.where(eye16, jnp.broadcast_to(total, (16, 128)), 0.0), axis=0, keepdims=True)
    tile0 = jnp.where(sub == 0, jnp.broadcast_to(total_row, (8, 128)), 0.0)
    for b in range(NB):
        tile0 = jnp.where(sub == 4 + b, par[b].astype(F32), tile0)
    table = (sub == jnp.broadcast_to(gid[...], (8, 128))).astype(F32)
    returns = ret[...]
    g_count = jnp.sum(table, axis=1, keepdims=True)
    g_sum = jnp.sum(table * returns, axis=1, keepdims=True)
    g_sq = jnp.sum(table * (returns * returns), axis=1, keepdims=True)
    tile1 = jnp.where(lane == 0, g_count, jnp.where(lane == 1, g_sum, jnp.where(lane == 2, g_sq, 0.0)))
    pk[seq, 0] = tile0
    pk[seq, 1] = tile1
    c_own = bc[...]
    for half in range(2):
        cg[half, second[half]] = c_own

    pl.semaphore_wait(barrier, 22)

    sent = []
    pk_in, c_in, u_in = [], [[], []], [[], []]
    for r in range(1, 16):
        copy = send(pk.at[seq], pk.at[seq], pk_s.at[r], pk_r.at[r], {"seq": (seq + r) % 16})
        pk_in.append(copy)
    sent += pk_in
    ORDER = (1, 3, 2)
    for half in range(2):
        s = second[half]
        for r in ORDER:
            peer = at(half, first[half], (s + r) % SIDE)
            c_in[half].append(
                send(cg.at[half, s], cg.at[half, s], c_s.at[half, r], c_r.at[half, r], {"seq": peer})
            )
    for c in range(NCH):
        for half in range(2):
            f = first[half]
            copies = {}
            for r in ORDER:
                peer = at(half, (f + r) % SIDE, second[half])
                copies[r] = send(
                    ug.at[half, c, f], ug.at[half, c, f], u_s.at[half, c, r], u_r.at[half, c, r], {"seq": peer}
                )
            u_in[half].append(copies)

    lift_e[...] = mm(stack_t[:, 32:64], spread32)
    einv_e[...] = mm(stack_t[:, 64:96], spread32)
    skip_e = jnp.sum(column(skip[...], LOCAL_HEADS) * spread16, axis=0, keepdims=True)
    gain_e = gain[...]
    scores = lax.dot_general(c_own, bb[...], (((1,), (1,)), ((), ())), preferred_element_type=F32)
    lower = upto_seg.T
    scores = (scores * lower).astype(BF16)
    smat[...] = scores
    x_own = bx[...].astype(F32)
    inner = mm(scores, (x_own * einv_e[...]).astype(BF16))
    y_s[...] = inner * lift_e[...] + skip_e * x_own
    z = bz[...].astype(F32)
    sz_s[...] = z / (1.0 + jnp.exp(-z))

    for copy in pk_in:
        copy.wait_recv()
    totals = pk[:, 0, 0, :]
    low16 = (iota((16, 16), 0) >= iota((16, 16), 1)).astype(F32)
    t_cum = jnp.dot(low16, totals, precision=HIGH, preferred_element_type=F32)
    t_e = jnp.dot(t_cum[:, :16], spread16, precision=HIGH, preferred_element_type=F32)
    for half in range(2):
        f0, s0 = first[half], second[half]
        parent = jnp.concatenate([pk[at(half, f0, s), 0, 4:8, :] for s in range(SIDE)], axis=0)
        onehot = (parent == iota((16, 128), 1).astype(F32)).astype(F32)
        lo = half * HALF
        t_half = t_e[:, lo : lo + HALF]
        t_par = jnp.dot(onehot[:, :16], t_half, precision=HIGH, preferred_element_type=F32)
        p_col = parent[:, 0:1]
        for f in range(SIDE):
            j = at(half, f, s0)
            pick = (iota((16, HALF), 0) == j).astype(F32)
            t_j = jnp.sum(t_half * pick, axis=0, keepdims=True)
            w = jnp.where(p_col >= j.astype(F32), jnp.exp(jnp.minimum(t_par - t_j, 0.0)), 0.0)
            for s in range(SIDE):
                wt[half, f, s, 0:4] = w[4 * s : 4 * s + 4]
    stats = pk[0, 1]
    for k in range(1, 16):
        stats = stats + pk[k, 1]
    floor_count = jnp.maximum(stats[:, 0:1], 1.0)
    mean = stats[:, 1:2] / floor_count
    spread = jnp.sqrt(stats[:, 2:3] / floor_count - mean * mean + 1.0)
    mean_row = jnp.sum(table * mean, axis=0, keepdims=True)
    spread_row = jnp.sum(table * spread, axis=0, keepdims=True)
    adv_row = (returns - mean_row) / spread_row

    for half in range(2):
        for copy in c_in[half]:
            copy.wait_recv()
    y_in = [[], []]
    for c in range(NCH):
        for half in range(2):
            f0, s0 = first[half], second[half]
            cs = slice(c * CW, (c + 1) * CW)
            for n, r in enumerate((0, 1, 3, 2)):
                f = (f0 + r) % SIDE
                if r:
                    u_in[half][c][(SIDE - r) % SIDE].wait_recv()
                u = ug[half, c, f]
                copies = {}
                for q in (2, 1, 3, 0):
                    s = (s0 + q) % SIDE
                    w = rows_to_tokens(wt[half, f, s, :, cs], CW)
                    part = mm(cg[half, s], u) * w
                    if n:
                        part = part + acc[q]
                    if n < 3:
                        acc[q] = part
                    elif q:
                        yp[half, c, q] = part.astype(BF16)
                        copies[q] = send(
                            yp.at[half, c, q],
                            yr.at[half, c, q],
                            y_ss.at[half, c, q],
                            y_rs.at[half, c, q],
                            {"seq": at(half, f0, s)},
                        )
                    else:
                        lo = half * HALF + c * CW
                        y_s[:, lo : lo + CW] = y_s[:, lo : lo + CW] + part * lift_e[:, lo : lo + CW]
            y_in[half].append(copies)

    for half in range(2):
        for s in range(SIDE):
            ct[half, s] = cg[half, s].astype(F32).T.astype(BF16)

    sq = jnp.zeros((BLOCK, 128), F32)
    al = jnp.zeros((BLOCK, 128), F32)
    for c in range(NCH):
        for half in range(2):
            lo = half * HALF + c * CW
            ws = slice(lo, lo + CW)
            got = None
            for q in (1, 3, 2):
                y_in[half][c][q].wait_recv()
                v = yr[half, c, q].astype(F32)
                got = v if got is None else got + v
            gated = (y_s[:, ws] + got * lift_e[:, ws]) * sz_s[:, ws]
            gated_s[:, ws] = gated
            squares = gated * gated
            inner = og[:, ws].astype(F32) * gain_e[:, ws] * gated
            for k in range(CW // 128):
                sq = sq + squares[:, 128 * k : 128 * k + 128]
                al = al + inner[:, 128 * k : 128 * k + 128]
    sq_row = jnp.sum(sq.T, axis=0, keepdims=True)
    al_row = jnp.sum(al.T, axis=0, keepdims=True)
    ar[head] = jnp.where(sub == 0, sq_row, jnp.where(sub == 1, al_row, 0.0))
    ar_in = [
        send(ar.at[head], ar.at[head], ar_s.at[r], ar_r.at[r], {"head": (head + r) % 8}) for r in (4, 3, 5, 2, 6, 7, 1)
    ]
    for copy in ar_in:
        copy.wait_recv()
    sums = ar[0]
    for k in range(1, 8):
        sums = sums + ar[k]
    scale = lax.rsqrt(sums[0:1] / (HEADS * HEAD_DIM) + EPSILON)
    along = adv_row * sums[1:2]
    kappa = scale * scale * scale * along / (HEADS * HEAD_DIM)
    sub128 = iota((128, 128), 0)
    rows = jnp.where(sub128 == 0, scale, jnp.where(sub128 == 1, scale * adv_row, jnp.where(sub128 == 2, kappa, 0.0)))
    cols = rows.T
    scale_c, push_c, kappa_c = cols[:, 0:1], cols[:, 1:2], cols[:, 2:3]

    d_in = [[], []]
    for c in range(NCH):
        for half in range(2):
            lo = half * HALF + c * CW
            ws = slice(lo, lo + CW)
            dy = (push_c * (og[:, ws].astype(F32) * gain_e[:, ws]) - kappa_c * gated_s[:, ws]) * sz_s[:, ws]
            dy_s[:, ws] = dy
            f0, s0 = first[half], second[half]
            dg[half, c, s0] = (dy * lift_e[:, ws]).astype(BF16)
            copies = {}
            for r in ORDER:
                copies[r] = send(
                    dg.at[half, c, s0],
                    dg.at[half, c, s0],
                    d_s.at[half, c, r],
                    d_r.at[half, c, r],
                    {"seq": at(half, f0, (s0 + r) % SIDE)},
                )
            d_in[half].append(copies)

    scores_t = smat[...].astype(F32).T.astype(BF16)
    for c in range(NCH):
        for half in range(2):
            lo = half * HALF + c * CW
            ws = slice(lo, lo + CW)
            back = mm(scores_t, dg[half, c, second[half]]) * einv_e[:, ws] + skip_e[:, ws] * dy_s[:, ws]
            grad_o[:, ws] = back.astype(BF16)
    out_o[...] = (gated_s[...] * scale_c * gain_e).astype(BF16)

    g_in = [[], []]
    for c in range(NCH):
        for half in range(2):
            f0, s0 = first[half], second[half]
            cs = slice(c * CW, (c + 1) * CW)
            for n, r in enumerate((0, 1, 3, 2)):
                s = (s0 + r) % SIDE
                if r:
                    d_in[half][c][(SIDE - r) % SIDE].wait_recv()
                d = dg[half, c, s].astype(F32)
                copies = {}
                for q in (2, 1, 3, 0):
                    f = (f0 + q) % SIDE
                    w = rows_to_tokens(wt[half, f, s, :, cs], CW)
                    part = mm(ct[half, s], (d * w).astype(BF16))
                    if n:
                        part = part + acc[q]
                    if n < 3 or q == 0:
                        acc[q if n < 3 else 4 + half * NCH + c] = part
                    else:
                        gp[half, c, q] = part.astype(BF16)
                        copies[q] = send(
                            gp.at[half, c, q],
                            gr.at[half, c, q],
                            g_s.at[half, c, q],
                            g_r.at[half, c, q],
                            {"seq": at(half, f, s0)},
                        )
            g_in[half].append(copies)

    p_b = pb[...]
    for c in range(NCH):
        for half in range(2):
            lo = half * HALF + c * CW
            ws = slice(lo, lo + CW)
            g = acc[4 + half * NCH + c]
            for q in (1, 3, 2):
                g_in[half][c][q].wait_recv()
                g = g + gr[half, c, q].astype(F32)
            prompt_o[:, ws] = mm(p_b, g.astype(BF16)) * tail_e[:, ws]

    for copy in sent + ar_in:
        copy.wait_send()
    for half in range(2):
        for copy in c_in[half]:
            copy.wait_send()
        for group in (u_in, y_in, d_in, g_in):
            for copies in group[half]:
                for copy in copies.values():
                    copy.wait_send()


def local(
    prompt_x, prompt_b, prompt_dt, branch_x, branch_b, branch_c, branch_z, branch_dt,
    a_rate, d_skip, norm_gain, branch_parent, group_ids, returns, out_grad,
):
    vm = pl.BlockSpec(memory_space=pltpu.VMEM)
    sm = pl.BlockSpec(memory_space=pltpu.SMEM)
    dma = pltpu.SemaphoreType.DMA
    V = pltpu.VMEM
    return pl.pallas_call(
        kernel,
        out_shape=(
            jax.ShapeDtypeStruct((BLOCK, CH), BF16),
            jax.ShapeDtypeStruct((BLOCK, CH), BF16),
            jax.ShapeDtypeStruct((BLOCK, CH), F32),
        ),
        in_specs=[vm] * 11 + [sm] + [vm] * 3,
        out_specs=(vm, vm, vm),
        scratch_shapes=[
            V((16, 2, 8, 128), F32),
            V((8, 8, 128), F32),
            V((2, NCH, SIDE, STATE, CW), BF16),
            V((2, SIDE, BLOCK, STATE), BF16),
            V((2, SIDE, STATE, BLOCK), BF16),
            V((2, NCH, SIDE, BLOCK, CW), BF16),
            V((2, NCH, SIDE, BLOCK, CW), BF16),
            V((2, NCH, SIDE, BLOCK, CW), BF16),
            V((2, NCH, SIDE, STATE, CW), BF16),
            V((2, NCH, SIDE, STATE, CW), BF16),
            V((4 + 2 * NCH, BLOCK, CW), F32),
            V((2, SIDE, SIDE, 8, HALF), F32),
            V((BLOCK, CH), F32),
            V((BLOCK, CH), F32),
            V((BLOCK, CH), F32),
            V((BLOCK, BLOCK), BF16),
            V((BLOCK, CH), F32),
            V((BLOCK, CH), F32),
            V((BLOCK, CH), F32),
            V((BLOCK, CH), F32),
            dma((16,)), dma((16,)), dma((8,)), dma((8,)),
            dma((2, NCH, SIDE)), dma((2, NCH, SIDE)),
            dma((2, SIDE)), dma((2, SIDE)),
            dma((2, NCH, SIDE)), dma((2, NCH, SIDE)),
            dma((2, NCH, SIDE)), dma((2, NCH, SIDE)),
            dma((2, NCH, SIDE)), dma((2, NCH, SIDE)),
        ],
        compiler_params=pltpu.CompilerParams(
            collective_id=0, has_side_effects=True, vmem_limit_bytes=40 * 2**20
        ),
    )(
        prompt_x, prompt_b, prompt_dt, branch_x, branch_b, branch_c, branch_z, branch_dt,
        a_rate.reshape(1, -1), d_skip.reshape(1, -1), norm_gain.reshape(1, -1), branch_parent,
        group_ids.reshape(1, -1), returns.reshape(1, -1), out_grad,
    )


def solution(mesh):
    rows = P(("parts", "seq"), "head")
    steps = P("head", ("parts", "seq"))
    heads = P("head")
    tokens = P(("parts", "seq"))
    return jax.shard_map(
        local,
        mesh=mesh,
        in_specs=(
            rows, rows, steps, rows, rows, rows, rows, steps,
            heads, heads, heads, tokens, tokens, tokens, rows,
        ),
        out_specs=(rows, rows, rows),
        check_vma=False,
    )
```

```python
import functools

import jax
import jax.numpy as jnp
from jax import lax
from jax.experimental import pallas as pl
from jax.experimental.pallas import tpu as pltpu
from jax.sharding import PartitionSpec as P

HEADS = 128
HEAD_DIM = 64
STATE = 128
BLOCK = 128
SEG = 32
NB = 4
EPSILON = 1e-05
SIDE = 4
LOCAL_HEADS = 16
CH = 1024
HALF = 512
NCH = 2
CW = HALF // NCH
MESH_ID = pl.DeviceIdType.MESH
F32 = jnp.float32
BF16 = jnp.bfloat16
HIGH = lax.Precision.HIGHEST


def iota(shape, dim):
    return lax.broadcasted_iota(jnp.int32, shape, dim)


def column(row, n):
    eye = iota((n, n), 0) == iota((n, n), 1)
    return jnp.sum(jnp.where(eye, jnp.broadcast_to(row, (n, n)), 0.0), axis=1, keepdims=True)


def split(v):
    high = v.astype(BF16).astype(F32)
    return high, v - high


def mm(a, b):
    return jnp.dot(a, b, preferred_element_type=F32)


def rows_to_tokens(w, width):
    return jnp.concatenate([jnp.broadcast_to(w[b : b + 1], (SEG, width)) for b in range(NB)], axis=0)


def kernel(
    px_h, pb_h, pdt_h, bx_h, bb_h, bc_h, bz_h, bdt_h, rate_h, skip_h, gain_h, par_h, gid_h, ret_h, og_h,
    out_o, grad_o, prompt_o,
    px, pb, pdt, bx, bb, bc, bz, bdt, rate, skip, gain, par, gid, ret, og, in_sem,
    pk, ar, ug, cg, ct, yp, yr, dg, gp, gr, acc, wt, tail_e, lift_e, einv_e, smat, y_s, gated_s, sz_s, dy_s,
    pk_s, pk_r, ar_s, ar_r, u_s, u_r, c_s, c_r, y_ss, y_rs, d_s, d_r, g_s, g_r,
):
    seq = lax.axis_index("seq")
    head = lax.axis_index("head")
    yi, xi = seq // SIDE, seq % SIDE

    loads = {}
    for n, (name, src, dst) in enumerate((
        ("pdt", pdt_h, pdt), ("rate", rate_h, rate), ("px", px_h, px), ("pb", pb_h, pb), ("bdt", bdt_h, bdt),
        ("par", par_h, par), ("gid", gid_h, gid), ("ret", ret_h, ret), ("bc", bc_h, bc), ("skip", skip_h, skip),
        ("bb", bb_h, bb), ("bx", bx_h, bx), ("bz", bz_h, bz), ("gain", gain_h, gain), ("og", og_h, og),
    )):
        loads[name] = pltpu.make_async_copy(src, dst, in_sem.at[n])
        loads[name].start()

    def loaded(*names):
        for name in names:
            loads[name].wait()

    barrier = pltpu.get_barrier_semaphore()
    for r in range(1, 16):
        pl.semaphore_signal(barrier, inc=1, device_id={"seq": (seq + r) % 16}, device_id_type=MESH_ID)
    for r in range(1, 8):
        pl.semaphore_signal(barrier, inc=1, device_id={"head": (head + r) % 8}, device_id_type=MESH_ID)

    first = (xi, yi)
    second = (yi, xi)

    def at(half, f, s):
        return s * SIDE + f if half == 0 else f * SIDE + s

    def send(src, dst, s_sem, r_sem, device):
        copy = pltpu.make_async_remote_copy(
            src_ref=src, dst_ref=dst, send_sem=s_sem, recv_sem=r_sem, device_id=device, device_id_type=MESH_ID
        )
        copy.start()
        sent.append(copy)
        return copy

    sent = []

    def arrive(copy):
        copy.wait_recv()

    loaded("pdt", "rate", "bdt")
    rate_c = column(rate[...], LOCAL_HEADS)
    upto = (iota((BLOCK, BLOCK), 0) <= iota((BLOCK, BLOCK), 1)).astype(F32)
    same = (iota((BLOCK, BLOCK), 0) // SEG) == (iota((BLOCK, BLOCK), 1) // SEG)
    upto_seg = jnp.where(same, upto, 0.0)
    p_dt = pdt[...]
    running = jnp.dot(p_dt * (-rate_c), upto, precision=HIGH, preferred_element_type=F32)
    total = running[:, BLOCK - 1 :]
    tails = jnp.exp(total - running) * p_dt
    b_dt = bdt[...]
    cum = jnp.dot(b_dt * (-rate_c), upto_seg, precision=HIGH, preferred_element_type=F32)
    lift = jnp.exp(cum)
    einv = jnp.exp(-cum) * b_dt

    stack = jnp.concatenate(
        [*split(tails), *split(lift), *split(einv), jnp.zeros((32, BLOCK), F32)], axis=0
    )
    stack_t = stack.T.astype(BF16)
    spread32 = ((iota((32, CH), 0) & 15) == (iota((32, CH), 1) >> 6)).astype(BF16)
    spread16 = ((iota((16, CH), 0)) == (iota((16, CH), 1) >> 6)).astype(F32)
    te = mm(stack_t[:, 0:32], spread32)
    tail_e[...] = te
    loaded("px", "pb")
    xw = (px[...].astype(F32) * te).astype(BF16)
    pb_t = pb[...].astype(F32).T.astype(BF16)
    for half in range(2):
        for c in range(NCH):
            lo = half * HALF + c * CW
            ug[half, c, first[half]] = mm(pb_t, xw[:, lo : lo + CW]).astype(BF16)

    loaded("par", "gid", "ret", "bc")
    sub = iota((8, 128), 0)
    lane = iota((8, 128), 1)
    eye16 = iota((16, 128), 0) == iota((16, 128), 1)
    total_row = jnp.sum(jnp.where(eye16, jnp.broadcast_to(total, (16, 128)), 0.0), axis=0, keepdims=True)
    tile0 = jnp.where(sub == 0, jnp.broadcast_to(total_row, (8, 128)), 0.0)
    for b in range(NB):
        tile0 = jnp.where(sub == 4 + b, par[b].astype(F32), tile0)
    table = (sub == jnp.broadcast_to(gid[...], (8, 128))).astype(F32)
    returns = ret[...]
    g_count = jnp.sum(table, axis=1, keepdims=True)
    g_sum = jnp.sum(table * returns, axis=1, keepdims=True)
    g_sq = jnp.sum(table * (returns * returns), axis=1, keepdims=True)
    tile1 = jnp.where(lane == 0, g_count, jnp.where(lane == 1, g_sum, jnp.where(lane == 2, g_sq, 0.0)))
    pk[seq, 0] = tile0
    pk[seq, 1] = tile1
    c_own = bc[...]
    for half in range(2):
        cg[half, second[half]] = c_own

    pl.semaphore_wait(barrier, 22)

    pk_in, c_in, u_in = [], [[], []], [[], []]
    for r in range(1, 16):
        copy = send(pk.at[seq], pk.at[seq], pk_s.at[r], pk_r.at[r], {"seq": (seq + r) % 16})
        pk_in.append(copy)
    ORDER = (1, 3, 2)
    for half in range(2):
        s = second[half]
        for r in ORDER:
            peer = at(half, first[half], (s + r) % SIDE)
            c_in[half].append(
                send(cg.at[half, s], cg.at[half, s], c_s.at[half, r], c_r.at[half, r], {"seq": peer})
            )
    for c in range(NCH):
        for half in range(2):
            f = first[half]
            copies = {}
            for r in ORDER:
                peer = at(half, (f + r) % SIDE, second[half])
                copies[r] = send(
                    ug.at[half, c, f], ug.at[half, c, f], u_s.at[half, c, r], u_r.at[half, c, r], {"seq": peer}
                )
            u_in[half].append(copies)

    loaded("skip", "bb", "bx", "bz", "gain", "og")
    lift_e[...] = mm(stack_t[:, 32:64], spread32)
    einv_e[...] = mm(stack_t[:, 64:96], spread32)
    skip_e = jnp.sum(column(skip[...], LOCAL_HEADS) * spread16, axis=0, keepdims=True)
    gain_e = gain[...]
    scores = lax.dot_general(c_own, bb[...], (((1,), (1,)), ((), ())), preferred_element_type=F32)
    lower = upto_seg.T
    scores = (scores * lower).astype(BF16)
    smat[...] = scores
    x_own = bx[...].astype(F32)
    inner = mm(scores, (x_own * einv_e[...]).astype(BF16))
    y_s[...] = inner * lift_e[...] + skip_e * x_own
    z = bz[...].astype(F32)
    sz_s[...] = z / (1.0 + jnp.exp(-z))

    for copy in pk_in:
        arrive(copy)
    totals = pk[:, 0, 0, :]
    low16 = (iota((16, 16), 0) >= iota((16, 16), 1)).astype(F32)
    t_cum = jnp.dot(low16, totals, precision=HIGH, preferred_element_type=F32)
    t_e = jnp.dot(t_cum[:, :16], spread16, precision=HIGH, preferred_element_type=F32)
    for half in range(2):
        f0, s0 = first[half], second[half]
        parent = jnp.concatenate([pk[at(half, f0, s), 0, 4:8, :] for s in range(SIDE)], axis=0)
        onehot = (parent == iota((16, 128), 1).astype(F32)).astype(F32)
        lo = half * HALF
        t_half = t_e[:, lo : lo + HALF]
        t_par = jnp.dot(onehot[:, :16], t_half, precision=HIGH, preferred_element_type=F32)
        p_col = parent[:, 0:1]
        for f in range(SIDE):
            j = at(half, f, s0)
            pick = (iota((16, HALF), 0) == j).astype(F32)
            t_j = jnp.sum(t_half * pick, axis=0, keepdims=True)
            w = jnp.where(p_col >= j.astype(F32), jnp.exp(jnp.minimum(t_par - t_j, 0.0)), 0.0)
            for s in range(SIDE):
                wt[half, f, s, 0:4] = w[4 * s : 4 * s + 4]
    stats = pk[0, 1]
    for k in range(1, 16):
        stats = stats + pk[k, 1]
    floor_count = jnp.maximum(stats[:, 0:1], 1.0)
    mean = stats[:, 1:2] / floor_count
    spread = jnp.sqrt(stats[:, 2:3] / floor_count - mean * mean + 1.0)
    mean_row = jnp.sum(table * mean, axis=0, keepdims=True)
    spread_row = jnp.sum(table * spread, axis=0, keepdims=True)
    adv_row = (returns - mean_row) / spread_row

    for half in range(2):
        for copy in c_in[half]:
            arrive(copy)
    y_in = [[], []]
    for c in range(NCH):
        for half in range(2):
            f0, s0 = first[half], second[half]
            cs = slice(c * CW, (c + 1) * CW)
            for n, r in enumerate((0, 1, 3, 2)):
                f = (f0 + r) % SIDE
                if r:
                    arrive(u_in[half][c][(SIDE - r) % SIDE])
                u = ug[half, c, f]
                copies = {}
                for q in (2, 1, 3, 0):
                    s = (s0 + q) % SIDE
                    w = rows_to_tokens(wt[half, f, s, :, cs], CW)
                    part = mm(cg[half, s], u) * w
                    if n:
                        part = part + acc[q]
                    if n < 3:
                        acc[q] = part
                    elif q:
                        yp[half, c, q] = part.astype(BF16)
                        copies[q] = send(
                            yp.at[half, c, q],
                            yr.at[half, c, q],
                            y_ss.at[half, c, q],
                            y_rs.at[half, c, q],
                            {"seq": at(half, f0, s)},
                        )
                    else:
                        lo = half * HALF + c * CW
                        y_s[:, lo : lo + CW] = y_s[:, lo : lo + CW] + part * lift_e[:, lo : lo + CW]
            y_in[half].append(copies)

    for half in range(2):
        for s in range(SIDE):
            ct[half, s] = cg[half, s].astype(F32).T.astype(BF16)

    sq = jnp.zeros((BLOCK, 128), F32)
    al = jnp.zeros((BLOCK, 128), F32)
    for c in range(NCH):
        for half in range(2):
            lo = half * HALF + c * CW
            ws = slice(lo, lo + CW)
            got = None
            for q in (1, 3, 2):
                arrive(y_in[half][c][q])
                v = yr[half, c, q].astype(F32)
                got = v if got is None else got + v
            gated = (y_s[:, ws] + got * lift_e[:, ws]) * sz_s[:, ws]
            gated_s[:, ws] = gated
            squares = gated * gated
            inner = og[:, ws].astype(F32) * gain_e[:, ws] * gated
            for k in range(CW // 128):
                sq = sq + squares[:, 128 * k : 128 * k + 128]
                al = al + inner[:, 128 * k : 128 * k + 128]
    sq_row = jnp.sum(sq.T, axis=0, keepdims=True)
    al_row = jnp.sum(al.T, axis=0, keepdims=True)
    ar[head] = jnp.where(sub == 0, sq_row, jnp.where(sub == 1, al_row, 0.0))
    ar_in = [
        send(ar.at[head], ar.at[head], ar_s.at[r], ar_r.at[r], {"head": (head + r) % 8}) for r in (4, 3, 5, 2, 6, 7, 1)
    ]
    for copy in ar_in:
        arrive(copy)
    sums = ar[0]
    for k in range(1, 8):
        sums = sums + ar[k]
    scale = lax.rsqrt(sums[0:1] / (HEADS * HEAD_DIM) + EPSILON)
    along = adv_row * sums[1:2]
    kappa = scale * scale * scale * along / (HEADS * HEAD_DIM)
    sub128 = iota((128, 128), 0)
    rows = jnp.where(sub128 == 0, scale, jnp.where(sub128 == 1, scale * adv_row, jnp.where(sub128 == 2, kappa, 0.0)))
    cols = rows.T
    scale_c, push_c, kappa_c = cols[:, 0:1], cols[:, 1:2], cols[:, 2:3]

    d_in = [[], []]
    for c in range(NCH):
        for half in range(2):
            lo = half * HALF + c * CW
            ws = slice(lo, lo + CW)
            dy = (push_c * (og[:, ws].astype(F32) * gain_e[:, ws]) - kappa_c * gated_s[:, ws]) * sz_s[:, ws]
            dy_s[:, ws] = dy
            f0, s0 = first[half], second[half]
            dg[half, c, s0] = (dy * lift_e[:, ws]).astype(BF16)
            copies = {}
            for r in ORDER:
                copies[r] = send(
                    dg.at[half, c, s0],
                    dg.at[half, c, s0],
                    d_s.at[half, c, r],
                    d_r.at[half, c, r],
                    {"seq": at(half, f0, (s0 + r) % SIDE)},
                )
            d_in[half].append(copies)

    scores_t = smat[...].astype(F32).T.astype(BF16)
    for c in range(NCH):
        for half in range(2):
            lo = half * HALF + c * CW
            ws = slice(lo, lo + CW)
            back = mm(scores_t, dg[half, c, second[half]]) * einv_e[:, ws] + skip_e[:, ws] * dy_s[:, ws]
            grad_o[:, ws] = back.astype(BF16)
    out_o[...] = (gated_s[...] * scale_c * gain_e).astype(BF16)

    g_in = [[], []]
    for c in range(NCH):
        for half in range(2):
            f0, s0 = first[half], second[half]
            cs = slice(c * CW, (c + 1) * CW)
            for n, r in enumerate((0, 1, 3, 2)):
                s = (s0 + r) % SIDE
                if r:
                    arrive(d_in[half][c][(SIDE - r) % SIDE])
                d = dg[half, c, s].astype(F32)
                copies = {}
                for q in (2, 1, 3, 0):
                    f = (f0 + q) % SIDE
                    w = rows_to_tokens(wt[half, f, s, :, cs], CW)
                    part = mm(ct[half, s], (d * w).astype(BF16))
                    if n:
                        part = part + acc[q]
                    if n < 3 or q == 0:
                        acc[q if n < 3 else 4 + half * NCH + c] = part
                    else:
                        gp[half, c, q] = part.astype(BF16)
                        copies[q] = send(
                            gp.at[half, c, q],
                            gr.at[half, c, q],
                            g_s.at[half, c, q],
                            g_r.at[half, c, q],
                            {"seq": at(half, f, s0)},
                        )
            g_in[half].append(copies)

    p_b = pb[...]
    for c in range(NCH):
        for half in range(2):
            lo = half * HALF + c * CW
            ws = slice(lo, lo + CW)
            g = acc[4 + half * NCH + c]
            for q in (1, 3, 2):
                arrive(g_in[half][c][q])
                g = g + gr[half, c, q].astype(F32)
            prompt_o[:, ws] = mm(p_b, g.astype(BF16)) * tail_e[:, ws]

    for copy in sent:
        copy.wait_send()


PIECES = 4


def hand_over(a, b, c, a_out, b_out, c_out):
    a_out[...] = a[...]
    b_out[...] = b[...]
    c_out[...] = c[...]


def local(
    prompt_x, prompt_b, prompt_dt, branch_x, branch_b, branch_c, branch_z, branch_dt,
    a_rate, d_skip, norm_gain, branch_parent, group_ids, returns, out_grad,
):
    vm = pl.BlockSpec(memory_space=pltpu.VMEM)
    dma = pltpu.SemaphoreType.DMA
    V = pltpu.VMEM
    results = pl.pallas_call(
        kernel,
        out_shape=(
            jax.ShapeDtypeStruct((BLOCK, CH), BF16),
            jax.ShapeDtypeStruct((BLOCK, CH), BF16),
            jax.ShapeDtypeStruct((BLOCK, CH), F32),
        ),
        in_specs=[pl.BlockSpec(memory_space=pltpu.HBM)] * 15,
        out_specs=(vm, vm, vm),
        scratch_shapes=[
            V((BLOCK, CH), BF16), V((BLOCK, STATE), BF16), V((LOCAL_HEADS, BLOCK), F32),
            V((BLOCK, CH), BF16), V((BLOCK, STATE), BF16), V((BLOCK, STATE), BF16),
            V((BLOCK, CH), BF16), V((LOCAL_HEADS, BLOCK), F32),
            V((1, LOCAL_HEADS), F32), V((1, LOCAL_HEADS), F32), V((1, CH), F32),
            pltpu.SMEM((NB,), jnp.int32), V((1, BLOCK), jnp.int32), V((1, BLOCK), F32),
            V((BLOCK, CH), BF16),
            dma((15,)),
            V((16, 2, 8, 128), F32),
            V((8, 8, 128), F32),
            V((2, NCH, SIDE, STATE, CW), BF16),
            V((2, SIDE, BLOCK, STATE), BF16),
            V((2, SIDE, STATE, BLOCK), BF16),
            V((2, NCH, SIDE, BLOCK, CW), BF16),
            V((2, NCH, SIDE, BLOCK, CW), BF16),
            V((2, NCH, SIDE, BLOCK, CW), BF16),
            V((2, NCH, SIDE, STATE, CW), BF16),
            V((2, NCH, SIDE, STATE, CW), BF16),
            V((4 + 2 * NCH, BLOCK, CW), F32),
            V((2, SIDE, SIDE, 8, HALF), F32),
            V((BLOCK, CH), F32),
            V((BLOCK, CH), F32),
            V((BLOCK, CH), F32),
            V((BLOCK, BLOCK), BF16),
            V((BLOCK, CH), F32),
            V((BLOCK, CH), F32),
            V((BLOCK, CH), F32),
            V((BLOCK, CH), F32),
            dma((16,)), dma((16,)), dma((8,)), dma((8,)),
            dma((2, NCH, SIDE)), dma((2, NCH, SIDE)),
            dma((2, SIDE)), dma((2, SIDE)),
            dma((2, NCH, SIDE)), dma((2, NCH, SIDE)),
            dma((2, NCH, SIDE)), dma((2, NCH, SIDE)),
            dma((2, NCH, SIDE)), dma((2, NCH, SIDE)),
        ],
        compiler_params=pltpu.CompilerParams(
            collective_id=0, has_side_effects=True, vmem_limit_bytes=40 * 2**20
        ),
    )(*(pltpu.with_memory_space_constraint(v, pltpu.HBM) for v in (
        prompt_x, prompt_b, prompt_dt, branch_x, branch_b, branch_c, branch_z, branch_dt,
        a_rate.reshape(1, -1), d_skip.reshape(1, -1), norm_gain.reshape(1, -1), branch_parent,
        group_ids.reshape(1, -1), returns.reshape(1, -1), out_grad,
    )))
    hbm = pl.BlockSpec(memory_space=pltpu.HBM)
    return pl.pallas_call(
        hand_over,
        out_shape=tuple(jax.ShapeDtypeStruct(r.shape, r.dtype) for r in results),
        in_specs=[vm] * 3,
        out_specs=(vm,) * 3,
        compiler_params=pltpu.CompilerParams(vmem_limit_bytes=16 * 2**20),
    )(*results)


def solution(mesh):
    rows = P(("parts", "seq"), "head")
    steps = P("head", ("parts", "seq"))
    heads = P("head")
    tokens = P(("parts", "seq"))
    return jax.shard_map(
        local,
        mesh=mesh,
        in_specs=(
            rows, rows, steps, rows, rows, rows, rows, steps,
            heads, heads, heads, tokens, tokens, tokens, rows,
        ),
        out_specs=(rows, rows, rows),
        check_vma=False,
    )
```

```python
import functools

import jax
import jax.numpy as jnp
from jax import lax
from jax.experimental import pallas as pl
from jax.experimental.pallas import tpu as pltpu
from jax.sharding import PartitionSpec as P

HEADS = 128
HEAD_DIM = 64
STATE = 128
BLOCK = 128
SEG = 32
NB = 4
EPSILON = 1e-05
SIDE = 4
LOCAL_HEADS = 16
CH = 1024
HALF = 512
NCH = 2
CW = HALF // NCH
MESH_ID = pl.DeviceIdType.MESH
F32 = jnp.float32
BF16 = jnp.bfloat16
HIGH = lax.Precision.HIGHEST


def iota(shape, dim):
    return lax.broadcasted_iota(jnp.int32, shape, dim)


def column(row, n):
    eye = iota((n, n), 0) == iota((n, n), 1)
    return jnp.sum(jnp.where(eye, jnp.broadcast_to(row, (n, n)), 0.0), axis=1, keepdims=True)


def split(v):
    high = v.astype(BF16).astype(F32)
    return high, v - high


def mm(a, b):
    return jnp.dot(a, b, preferred_element_type=F32)


def rows_to_tokens(w, width):
    return jnp.concatenate([jnp.broadcast_to(w[b : b + 1], (SEG, width)) for b in range(NB)], axis=0)


def kernel(
    px_h, pb_h, pdt_h, bx_h, bb_h, bc_h, bz_h, bdt_h, rate_h, skip_h, gain_h, par_h, gid_h, ret_h, og_h,
    out_o, grad_o, prompt_o,
    px, pb, pdt, bx, bb, bc, bz, bdt, rate, skip, gain, par, gid, ret, og, in_sem,
    pk, ar, ug, cg, ct, yp, yr, dg, gp, gr, acc, wt, tail_e, lift_e, einv_e, smat, y_s, gated_s, sz_s, dy_s, og_s,
    pk_s, pk_r, ar_s, ar_r, u_s, u_r, c_s, c_r, y_ss, y_rs, d_s, d_r, g_s, g_r,
):
    seq = lax.axis_index("seq")
    head = lax.axis_index("head")
    yi, xi = seq // SIDE, seq % SIDE

    loads = {}
    for n, (name, src, dst) in enumerate((
        ("pdt", pdt_h, pdt), ("rate", rate_h, rate), ("px", px_h, px), ("pb", pb_h, pb), ("bdt", bdt_h, bdt),
        ("par", par_h, par), ("gid", gid_h, gid), ("ret", ret_h, ret), ("bc", bc_h, bc), ("skip", skip_h, skip),
        ("bb", bb_h, bb), ("bx", bx_h, bx), ("bz", bz_h, bz), ("gain", gain_h, gain), ("og", og_h, og),
    )):
        loads[name] = pltpu.make_async_copy(src, dst, in_sem.at[n])
        loads[name].start()

    def loaded(*names):
        for name in names:
            loads[name].wait()

    barrier = pltpu.get_barrier_semaphore()
    for r in range(1, SIDE):
        pl.semaphore_signal(
            barrier, inc=1, device_id={"seq": yi * SIDE + (xi + r) % SIDE}, device_id_type=MESH_ID
        )
        pl.semaphore_signal(
            barrier, inc=1, device_id={"seq": (yi + r) % SIDE * SIDE + xi}, device_id_type=MESH_ID
        )
    for r in range(1, 8):
        pl.semaphore_signal(barrier, inc=1, device_id={"head": (head + r) % 8}, device_id_type=MESH_ID)

    first = (xi, yi)
    second = (yi, xi)

    def at(half, f, s):
        return s * SIDE + f if half == 0 else f * SIDE + s

    def send(src, dst, s_sem, r_sem, device):
        copy = pltpu.make_async_remote_copy(
            src_ref=src, dst_ref=dst, send_sem=s_sem, recv_sem=r_sem, device_id=device, device_id_type=MESH_ID
        )
        copy.start()
        sent.append(copy)
        return copy

    sent = []

    def arrive(copy):
        copy.wait_recv()

    loaded("pdt", "rate", "bdt")
    rate_c = column(rate[...], LOCAL_HEADS)
    upto = (iota((BLOCK, BLOCK), 0) <= iota((BLOCK, BLOCK), 1)).astype(F32)
    same = (iota((BLOCK, BLOCK), 0) // SEG) == (iota((BLOCK, BLOCK), 1) // SEG)
    upto_seg = jnp.where(same, upto, 0.0)
    p_dt = pdt[...]
    running = jnp.dot(p_dt * (-rate_c), upto, precision=HIGH, preferred_element_type=F32)
    total = running[:, BLOCK - 1 :]
    tails = jnp.exp(total - running) * p_dt
    b_dt = bdt[...]
    cum = jnp.dot(b_dt * (-rate_c), upto_seg, precision=HIGH, preferred_element_type=F32)
    lift = jnp.exp(cum)
    einv = jnp.exp(-cum) * b_dt

    stack = jnp.concatenate(
        [*split(tails), *split(lift), *split(einv), jnp.zeros((32, BLOCK), F32)], axis=0
    )
    stack_t = stack.T.astype(BF16)
    spread32 = ((iota((32, CH), 0) & 15) == (iota((32, CH), 1) >> 6)).astype(BF16)
    spread16 = ((iota((16, CH), 0)) == (iota((16, CH), 1) >> 6)).astype(F32)
    te = mm(stack_t[:, 0:32], spread32)
    tail_e[...] = te
    loaded("px", "pb")
    xw = (px[...].astype(F32) * te).astype(BF16)
    pb_t = pb[...].astype(F32).T.astype(BF16)
    for half in range(2):
        for c in range(NCH):
            lo = half * HALF + c * CW
            ug[half, c, first[half]] = mm(pb_t, xw[:, lo : lo + CW]).astype(BF16)

    loaded("par", "gid", "ret", "bc")
    sub = iota((8, 128), 0)
    lane = iota((8, 128), 1)
    eye16 = iota((16, 128), 0) == iota((16, 128), 1)
    total_row = jnp.sum(jnp.where(eye16, jnp.broadcast_to(total, (16, 128)), 0.0), axis=0, keepdims=True)
    parents = jnp.zeros((8, 128), F32)
    for b in range(NB):
        parents = jnp.where(sub == 4 + b, par[b].astype(F32), parents)
    table = (sub == jnp.broadcast_to(gid[...], (8, 128))).astype(F32)
    returns = ret[...]
    g_count = jnp.sum(table, axis=1, keepdims=True)
    g_sum = jnp.sum(table * returns, axis=1, keepdims=True)
    g_sq = jnp.sum(table * (returns * returns), axis=1, keepdims=True)
    tile = jnp.where(sub == 0, jnp.broadcast_to(total_row, (8, 128)), 0.0)
    tile = jnp.where((lane >= 32) & (lane < 48), parents, tile)
    for n, value in enumerate((g_count, g_sum, g_sq)):
        tile = jnp.where(lane == 64 + n, value, tile)
    pk[yi, xi] = tile
    c_own = bc[...]
    for half in range(2):
        cg[half, second[half]] = c_own

    pl.semaphore_wait(barrier, 13)

    pk_in, c_in, u_in = [], [[], []], [[], []]
    for r in (2, 1, 3):
        peer = yi * SIDE + (xi + r) % SIDE
        pk_in.append(send(pk.at[yi, xi], pk.at[yi, xi], pk_s.at[0, r], pk_r.at[0, r], {"seq": peer}))
    ORDER = (1, 3, 2)
    for half in range(2):
        s = second[half]
        for r in ORDER:
            peer = at(half, first[half], (s + r) % SIDE)
            c_in[half].append(
                send(cg.at[half, s], cg.at[half, s], c_s.at[half, r], c_r.at[half, r], {"seq": peer})
            )
    def send_updates(c, distances):
        for half in range(2):
            f = first[half]
            if len(u_in[half]) == c:
                u_in[half].append({})
            copies = u_in[half][c]
            for r in distances:
                peer = at(half, (f + r) % SIDE, second[half])
                copies[r] = send(
                    ug.at[half, c, f], ug.at[half, c, f], u_s.at[half, c, r], u_r.at[half, c, r], {"seq": peer}
                )

    send_updates(0, (1, 3))

    loaded("skip", "bb", "bx", "bz", "gain", "og")
    lift_e[...] = mm(stack_t[:, 32:64], spread32)
    einv_e[...] = mm(stack_t[:, 64:96], spread32)
    skip_e = jnp.sum(column(skip[...], LOCAL_HEADS) * spread16, axis=0, keepdims=True)
    gain_e = gain[...]
    scores = lax.dot_general(c_own, bb[...], (((1,), (1,)), ((), ())), preferred_element_type=F32)
    lower = upto_seg.T
    scores = (scores * lower).astype(BF16)
    smat[...] = scores
    x_own = bx[...].astype(F32)
    inner = mm(scores, (x_own * einv_e[...]).astype(BF16))
    y_s[...] = inner * lift_e[...] + skip_e * x_own
    z = bz[...].astype(F32)
    sz_s[...] = z / (1.0 + jnp.exp(-z))

    for copy in pk_in:
        arrive(copy)
    pk_in = []
    for r in (2, 1, 3):
        peer = (yi + r) % SIDE * SIDE + xi
        pk_in.append(send(pk.at[yi], pk.at[yi], pk_s.at[1, r], pk_r.at[1, r], {"seq": peer}))
    send_updates(0, (2,))
    for c in range(1, NCH):
        send_updates(c, ORDER)
    og_s[...] = og[...].astype(F32) * gain_e

    for copy in pk_in:
        arrive(copy)
    totals = jnp.concatenate([pk[k // SIDE, k % SIDE, 0:1, :] for k in range(16)], axis=0)
    low16 = (iota((16, 16), 0) >= iota((16, 16), 1)).astype(F32)
    t_cum = jnp.dot(low16, totals, precision=HIGH, preferred_element_type=F32)
    t_e = jnp.dot(t_cum[:, :16], spread16, precision=HIGH, preferred_element_type=F32)
    for half in range(2):
        f0, s0 = first[half], second[half]
        parent = jnp.concatenate([(pk[s, f0] if half == 0 else pk[f0, s])[4:8] for s in range(SIDE)], axis=0)
        onehot = (parent[:, 32:48] == iota((16, 16), 1).astype(F32)).astype(F32)
        lo = half * HALF
        t_half = t_e[:, lo : lo + HALF]
        t_par = jnp.dot(onehot, t_half, precision=HIGH, preferred_element_type=F32)
        p_col = parent[:, 32:33]
        for f in range(SIDE):
            j = at(half, f, s0)
            pick = (iota((16, HALF), 0) == j).astype(F32)
            t_j = jnp.sum(t_half * pick, axis=0, keepdims=True)
            w = jnp.where(p_col >= j.astype(F32), jnp.exp(jnp.minimum(t_par - t_j, 0.0)), 0.0)
            for s in range(SIDE):
                wt[half, f, s, 0:4] = w[4 * s : 4 * s + 4]
    stats = pk[0, 0]
    for k in range(1, 16):
        stats = stats + pk[k // SIDE, k % SIDE]
    floor_count = jnp.maximum(stats[:, 64:65], 1.0)
    mean = stats[:, 65:66] / floor_count
    spread = jnp.sqrt(stats[:, 66:67] / floor_count - mean * mean + 1.0)
    mean_row = jnp.sum(table * mean, axis=0, keepdims=True)
    spread_row = jnp.sum(table * spread, axis=0, keepdims=True)
    adv_row = (returns - mean_row) / spread_row

    for half in range(2):
        for copy in c_in[half]:
            arrive(copy)
    y_in = [[], []]
    for c in range(NCH):
        for half in range(2):
            f0, s0 = first[half], second[half]
            cs = slice(c * CW, (c + 1) * CW)
            for n, r in enumerate((0, 1, 3, 2)):
                f = (f0 + r) % SIDE
                if r:
                    arrive(u_in[half][c][(SIDE - r) % SIDE])
                u = ug[half, c, f]
                copies = {}
                for q in (2, 1, 3, 0):
                    s = (s0 + q) % SIDE
                    w = rows_to_tokens(wt[half, f, s, :, cs], CW)
                    part = mm(cg[half, s], u) * w
                    if n:
                        part = part + acc[q]
                    if n < 3:
                        acc[q] = part
                    elif q:
                        yp[half, c, q] = part.astype(BF16)
                        copies[q] = send(
                            yp.at[half, c, q],
                            yr.at[half, c, q],
                            y_ss.at[half, c, q],
                            y_rs.at[half, c, q],
                            {"seq": at(half, f0, s)},
                        )
                    else:
                        lo = half * HALF + c * CW
                        y_s[:, lo : lo + CW] = y_s[:, lo : lo + CW] + part * lift_e[:, lo : lo + CW]
            y_in[half].append(copies)

    for half in range(2):
        for s in range(SIDE):
            ct[half, s] = cg[half, s].astype(F32).T.astype(BF16)

    sq = jnp.zeros((BLOCK, 128), F32)
    al = jnp.zeros((BLOCK, 128), F32)
    for c in range(NCH):
        for half in range(2):
            lo = half * HALF + c * CW
            ws = slice(lo, lo + CW)
            got = None
            for q in (1, 3, 2):
                arrive(y_in[half][c][q])
                v = yr[half, c, q].astype(F32)
                got = v if got is None else got + v
            gated = (y_s[:, ws] + got * lift_e[:, ws]) * sz_s[:, ws]
            gated_s[:, ws] = gated
            squares = gated * gated
            inner = og_s[:, ws] * gated
            for k in range(CW // 128):
                sq = sq + squares[:, 128 * k : 128 * k + 128]
                al = al + inner[:, 128 * k : 128 * k + 128]
    sq_row = jnp.sum(sq.T, axis=0, keepdims=True)
    al_row = jnp.sum(al.T, axis=0, keepdims=True)
    ar[head] = jnp.where(sub == 0, sq_row, jnp.where(sub == 1, al_row, 0.0))
    ar_in = [
        send(ar.at[head], ar.at[head], ar_s.at[r], ar_r.at[r], {"head": (head + r) % 8}) for r in (4, 3, 5, 2, 6, 7, 1)
    ]
    for copy in ar_in:
        arrive(copy)
    sums = ar[0]
    for k in range(1, 8):
        sums = sums + ar[k]
    scale = lax.rsqrt(sums[0:1] / (HEADS * HEAD_DIM) + EPSILON)
    along = adv_row * sums[1:2]
    kappa = scale * scale * scale * along / (HEADS * HEAD_DIM)
    sub128 = iota((128, 128), 0)
    rows = jnp.where(sub128 == 0, scale, jnp.where(sub128 == 1, scale * adv_row, jnp.where(sub128 == 2, kappa, 0.0)))
    cols = rows.T
    scale_c, push_c, kappa_c = cols[:, 0:1], cols[:, 1:2], cols[:, 2:3]

    d_in = [[], []]
    for c in range(NCH):
        for half in range(2):
            lo = half * HALF + c * CW
            ws = slice(lo, lo + CW)
            dy = (push_c * og_s[:, ws] - kappa_c * gated_s[:, ws]) * sz_s[:, ws]
            dy_s[:, ws] = dy
            f0, s0 = first[half], second[half]
            dg[half, c, s0] = (dy * lift_e[:, ws]).astype(BF16)
            copies = {}
            for r in ORDER:
                copies[r] = send(
                    dg.at[half, c, s0],
                    dg.at[half, c, s0],
                    d_s.at[half, c, r],
                    d_r.at[half, c, r],
                    {"seq": at(half, f0, (s0 + r) % SIDE)},
                )
            d_in[half].append(copies)

    scores_t = smat[...].astype(F32).T.astype(BF16)
    for c in range(NCH):
        for half in range(2):
            lo = half * HALF + c * CW
            ws = slice(lo, lo + CW)
            back = mm(scores_t, dg[half, c, second[half]]) * einv_e[:, ws] + skip_e[:, ws] * dy_s[:, ws]
            grad_o[:, ws] = back.astype(BF16)
    out_o[...] = (gated_s[...] * scale_c * gain_e).astype(BF16)

    g_in = [[], []]
    for c in range(NCH):
        for half in range(2):
            f0, s0 = first[half], second[half]
            cs = slice(c * CW, (c + 1) * CW)
            for n, r in enumerate((0, 1, 3, 2)):
                s = (s0 + r) % SIDE
                if r:
                    arrive(d_in[half][c][(SIDE - r) % SIDE])
                d = dg[half, c, s].astype(F32)
                copies = {}
                for q in (2, 1, 3, 0):
                    f = (f0 + q) % SIDE
                    w = rows_to_tokens(wt[half, f, s, :, cs], CW)
                    part = mm(ct[half, s], (d * w).astype(BF16))
                    if n:
                        part = part + acc[q]
                    if n < 3 or q == 0:
                        acc[q if n < 3 else 4 + half * NCH + c] = part
                    else:
                        gp[half, c, q] = part.astype(BF16)
                        copies[q] = send(
                            gp.at[half, c, q],
                            gr.at[half, c, q],
                            g_s.at[half, c, q],
                            g_r.at[half, c, q],
                            {"seq": at(half, f, s0)},
                        )
            g_in[half].append(copies)

    p_b = pb[...]
    for c in range(NCH):
        for half in range(2):
            lo = half * HALF + c * CW
            ws = slice(lo, lo + CW)
            g = acc[4 + half * NCH + c]
            for q in (1, 3, 2):
                arrive(g_in[half][c][q])
                g = g + gr[half, c, q].astype(F32)
            prompt_o[:, ws] = mm(p_b, g.astype(BF16)) * tail_e[:, ws]

    for copy in sent:
        copy.wait_send()


PIECES = 4


def hand_over(a, b, c, a_out, b_out, c_out):
    a_out[...] = a[...]
    b_out[...] = b[...]
    c_out[...] = c[...]


def local(
    prompt_x, prompt_b, prompt_dt, branch_x, branch_b, branch_c, branch_z, branch_dt,
    a_rate, d_skip, norm_gain, branch_parent, group_ids, returns, out_grad,
):
    vm = pl.BlockSpec(memory_space=pltpu.VMEM)
    dma = pltpu.SemaphoreType.DMA
    V = pltpu.VMEM
    results = pl.pallas_call(
        kernel,
        out_shape=(
            jax.ShapeDtypeStruct((BLOCK, CH), BF16),
            jax.ShapeDtypeStruct((BLOCK, CH), BF16),
            jax.ShapeDtypeStruct((BLOCK, CH), F32),
        ),
        in_specs=[pl.BlockSpec(memory_space=pltpu.HBM)] * 15,
        out_specs=(vm, vm, vm),
        scratch_shapes=[
            V((BLOCK, CH), BF16), V((BLOCK, STATE), BF16), V((LOCAL_HEADS, BLOCK), F32),
            V((BLOCK, CH), BF16), V((BLOCK, STATE), BF16), V((BLOCK, STATE), BF16),
            V((BLOCK, CH), BF16), V((LOCAL_HEADS, BLOCK), F32),
            V((1, LOCAL_HEADS), F32), V((1, LOCAL_HEADS), F32), V((1, CH), F32),
            pltpu.SMEM((NB,), jnp.int32), V((1, BLOCK), jnp.int32), V((1, BLOCK), F32),
            V((BLOCK, CH), BF16),
            dma((15,)),
            V((SIDE, SIDE, 8, 128), F32),
            V((8, 8, 128), F32),
            V((2, NCH, SIDE, STATE, CW), BF16),
            V((2, SIDE, BLOCK, STATE), BF16),
            V((2, SIDE, STATE, BLOCK), BF16),
            V((2, NCH, SIDE, BLOCK, CW), BF16),
            V((2, NCH, SIDE, BLOCK, CW), BF16),
            V((2, NCH, SIDE, BLOCK, CW), BF16),
            V((2, NCH, SIDE, STATE, CW), BF16),
            V((2, NCH, SIDE, STATE, CW), BF16),
            V((4 + 2 * NCH, BLOCK, CW), F32),
            V((2, SIDE, SIDE, 8, HALF), F32),
            V((BLOCK, CH), F32),
            V((BLOCK, CH), F32),
            V((BLOCK, CH), F32),
            V((BLOCK, BLOCK), BF16),
            V((BLOCK, CH), F32),
            V((BLOCK, CH), F32),
            V((BLOCK, CH), F32),
            V((BLOCK, CH), F32),
            V((BLOCK, CH), F32),
            dma((2, SIDE)), dma((2, SIDE)), dma((8,)), dma((8,)),
            dma((2, NCH, SIDE)), dma((2, NCH, SIDE)),
            dma((2, SIDE)), dma((2, SIDE)),
            dma((2, NCH, SIDE)), dma((2, NCH, SIDE)),
            dma((2, NCH, SIDE)), dma((2, NCH, SIDE)),
            dma((2, NCH, SIDE)), dma((2, NCH, SIDE)),
        ],
        compiler_params=pltpu.CompilerParams(
            collective_id=0, has_side_effects=True, vmem_limit_bytes=40 * 2**20
        ),
    )(*(pltpu.with_memory_space_constraint(v, pltpu.HBM) for v in (
        prompt_x, prompt_b, prompt_dt, branch_x, branch_b, branch_c, branch_z, branch_dt,
        a_rate.reshape(1, -1), d_skip.reshape(1, -1), norm_gain.reshape(1, -1), branch_parent,
        group_ids.reshape(1, -1), returns.reshape(1, -1), out_grad,
    )))
    hbm = pl.BlockSpec(memory_space=pltpu.HBM)
    return pl.pallas_call(
        hand_over,
        out_shape=tuple(jax.ShapeDtypeStruct(r.shape, r.dtype) for r in results),
        in_specs=[vm] * 3,
        out_specs=(vm,) * 3,
        compiler_params=pltpu.CompilerParams(vmem_limit_bytes=16 * 2**20),
    )(*results)


def solution(mesh):
    rows = P(("parts", "seq"), "head")
    steps = P("head", ("parts", "seq"))
    heads = P("head")
    tokens = P(("parts", "seq"))
    return jax.shard_map(
        local,
        mesh=mesh,
        in_specs=(
            rows, rows, steps, rows, rows, rows, rows, steps,
            heads, heads, heads, tokens, tokens, tokens, rows,
        ),
        out_specs=(rows, rows, rows),
        check_vma=False,
    )
```

```python
import functools

import jax
import jax.numpy as jnp
from jax import lax
from jax.experimental import pallas as pl
from jax.experimental.pallas import tpu as pltpu
from jax.sharding import PartitionSpec as P

HEADS = 128
HEAD_DIM = 64
STATE = 128
BLOCK = 128
SEG = 32
NB = 4
EPSILON = 1e-05
SIDE = 4
LOCAL_HEADS = 16
CH = 1024
HALF = 512
NCH = 2
EARLY = 1
CW = HALF // NCH
MESH_ID = pl.DeviceIdType.MESH
F32 = jnp.float32
BF16 = jnp.bfloat16
HIGH = lax.Precision.HIGHEST


def iota(shape, dim):
    return lax.broadcasted_iota(jnp.int32, shape, dim)


def column(row, n):
    eye = iota((n, n), 0) == iota((n, n), 1)
    return jnp.sum(jnp.where(eye, jnp.broadcast_to(row, (n, n)), 0.0), axis=1, keepdims=True)


def split(v):
    high = v.astype(BF16).astype(F32)
    return high, v - high


def mm(a, b):
    return jnp.dot(a, b, preferred_element_type=F32)


def rows_to_tokens(w, width):
    return jnp.concatenate([jnp.broadcast_to(w[b : b + 1], (SEG, width)) for b in range(NB)], axis=0)


def kernel(
    px_h, pb_h, pdt_h, bx_h, bb_h, bc_h, bz_h, bdt_h, rate_h, skip_h, gain_h, par_h, gid_h, ret_h, og_h,
    out_o, grad_o, prompt_o,
    px, pb, pdt, bx, bb, bc, bz, bdt, rate, skip, gain, par, gid, ret, og, in_sem,
    pk, ar, ug, cg, ct, yp, yr, dg, gp, gr, acc, wt, tail_e, lift_e, einv_e, smat, y_s, gated_s, sz_s, dy_s, og_s, pg, qg, sg, sg_c,
    pg_s, pg_r, qg_s, qg_r, sg_s, sg_r,
    pk_s, pk_r, ar_s, ar_r, u_s, u_r, c_s, c_r, y_ss, y_rs, d_s, d_r, g_s, g_r,
):
    seq = lax.axis_index("seq")
    head = lax.axis_index("head")
    yi, xi = seq // SIDE, seq % SIDE

    loads = {}
    for n, (name, src, dst) in enumerate((
        ("pdt", pdt_h, pdt), ("rate", rate_h, rate), ("px", px_h, px), ("pb", pb_h, pb), ("bdt", bdt_h, bdt),
        ("par", par_h, par), ("gid", gid_h, gid), ("ret", ret_h, ret), ("bc", bc_h, bc), ("skip", skip_h, skip),
        ("bb", bb_h, bb), ("bx", bx_h, bx), ("bz", bz_h, bz), ("gain", gain_h, gain), ("og", og_h, og),
    )):
        loads[name] = pltpu.make_async_copy(src, dst, in_sem.at[n])
        loads[name].start()

    def loaded(*names):
        for name in names:
            loads[name].wait()

    barrier = pltpu.get_barrier_semaphore()
    for r in range(1, SIDE):
        pl.semaphore_signal(
            barrier, inc=1, device_id={"seq": yi * SIDE + (xi + r) % SIDE}, device_id_type=MESH_ID
        )
        pl.semaphore_signal(
            barrier, inc=1, device_id={"seq": (yi + r) % SIDE * SIDE + xi}, device_id_type=MESH_ID
        )
    for r in range(1, 8):
        pl.semaphore_signal(barrier, inc=1, device_id={"head": (head + r) % 8}, device_id_type=MESH_ID)

    first = (xi, yi)
    second = (yi, xi)

    def at(half, f, s):
        return s * SIDE + f if half == 0 else f * SIDE + s

    def send(src, dst, s_sem, r_sem, device):
        copy = pltpu.make_async_remote_copy(
            src_ref=src, dst_ref=dst, send_sem=s_sem, recv_sem=r_sem, device_id=device, device_id_type=MESH_ID
        )
        copy.start()
        sent.append(copy)
        return copy

    sent = []

    def arrive(copy):
        copy.wait_recv()

    loaded("pdt", "rate", "bdt")
    rate_c = column(rate[...], LOCAL_HEADS)
    upto = (iota((BLOCK, BLOCK), 0) <= iota((BLOCK, BLOCK), 1)).astype(F32)
    same = (iota((BLOCK, BLOCK), 0) // SEG) == (iota((BLOCK, BLOCK), 1) // SEG)
    upto_seg = jnp.where(same, upto, 0.0)
    p_dt = pdt[...]
    running = jnp.dot(p_dt * (-rate_c), upto, precision=HIGH, preferred_element_type=F32)
    total = running[:, BLOCK - 1 :]
    tails = jnp.exp(total - running) * p_dt
    b_dt = bdt[...]
    cum = jnp.dot(b_dt * (-rate_c), upto_seg, precision=HIGH, preferred_element_type=F32)
    lift = jnp.exp(cum)
    einv = jnp.exp(-cum) * b_dt

    stack = jnp.concatenate(
        [*split(tails), *split(lift), *split(einv), jnp.zeros((32, BLOCK), F32)], axis=0
    )
    stack_t = stack.T.astype(BF16)
    spread32 = ((iota((32, CH), 0) & 15) == (iota((32, CH), 1) >> 6)).astype(BF16)
    spread16 = ((iota((16, CH), 0)) == (iota((16, CH), 1) >> 6)).astype(F32)
    te = mm(stack_t[:, 0:32], spread32)
    tail_e[...] = te
    loaded("px", "pb")
    xw = (px[...].astype(F32) * te).astype(BF16)
    pb_t = pb[...].astype(F32).T.astype(BF16)
    for half in range(2):
        for c in range(NCH):
            lo = half * HALF + c * CW
            ug[half, c, first[half]] = mm(pb_t, xw[:, lo : lo + CW]).astype(BF16)

    loaded("par", "gid", "ret", "bc")
    sub = iota((8, 128), 0)
    lane = iota((8, 128), 1)
    eye16 = iota((16, 128), 0) == iota((16, 128), 1)
    total_row = jnp.sum(jnp.where(eye16, jnp.broadcast_to(total, (16, 128)), 0.0), axis=0, keepdims=True)
    parents = jnp.zeros((8, 128), F32)
    for b in range(NB):
        parents = jnp.where(sub == 4 + b, par[b].astype(F32), parents)
    table = (sub == jnp.broadcast_to(gid[...], (8, 128))).astype(F32)
    returns = ret[...]
    g_count = jnp.sum(table, axis=1, keepdims=True)
    g_sum = jnp.sum(table * returns, axis=1, keepdims=True)
    g_sq = jnp.sum(table * (returns * returns), axis=1, keepdims=True)
    tile = jnp.where(sub == 0, jnp.broadcast_to(total_row, (8, 128)), 0.0)
    tile = jnp.where((lane >= 32) & (lane < 48), parents, tile)
    for n, value in enumerate((g_count, g_sum, g_sq)):
        tile = jnp.where(lane == 64 + n, value, tile)
    pk[yi, xi] = tile
    c_own = bc[...]
    for half in range(2):
        cg[half, second[half]] = c_own

    pl.semaphore_wait(barrier, 13)

    pk_in, c_in, u_in = [], [[], []], [[], []]
    for r in (2, 1, 3):
        peer = yi * SIDE + (xi + r) % SIDE
        pk_in.append(send(pk.at[yi, xi], pk.at[yi, xi], pk_s.at[0, r], pk_r.at[0, r], {"seq": peer}))
    ORDER = (1, 3, 2)
    for half in range(2):
        s = second[half]
        for r in ORDER:
            peer = at(half, first[half], (s + r) % SIDE)
            c_in[half].append(
                send(cg.at[half, s], cg.at[half, s], c_s.at[half, r], c_r.at[half, r], {"seq": peer})
            )
    def send_updates(c, distances):
        for half in range(2):
            f = first[half]
            if len(u_in[half]) == c:
                u_in[half].append({})
            copies = u_in[half][c]
            for r in distances:
                peer = at(half, (f + r) % SIDE, second[half])
                copies[r] = send(
                    ug.at[half, c, f], ug.at[half, c, f], u_s.at[half, c, r], u_r.at[half, c, r], {"seq": peer}
                )

    send_updates(0, (1, 3))

    loaded("skip", "bb", "bx", "bz", "gain", "og")
    lift_e[...] = mm(stack_t[:, 32:64], spread32)
    einv_e[...] = mm(stack_t[:, 64:96], spread32)
    skip_e = jnp.sum(column(skip[...], LOCAL_HEADS) * spread16, axis=0, keepdims=True)
    gain_e = gain[...]
    scores = lax.dot_general(c_own, bb[...], (((1,), (1,)), ((), ())), preferred_element_type=F32)
    lower = upto_seg.T
    scores = (scores * lower).astype(BF16)
    smat[...] = scores
    x_own = bx[...].astype(F32)
    inner = mm(scores, (x_own * einv_e[...]).astype(BF16))
    y_s[...] = inner * lift_e[...] + skip_e * x_own
    z = bz[...].astype(F32)
    sz_s[...] = z / (1.0 + jnp.exp(-z))

    for copy in pk_in:
        arrive(copy)
    pk_in = []
    for r in (2, 1, 3):
        peer = (yi + r) % SIDE * SIDE + xi
        pk_in.append(send(pk.at[yi], pk.at[yi], pk_s.at[1, r], pk_r.at[1, r], {"seq": peer}))
    send_updates(0, (2,))
    for c in range(1, NCH):
        send_updates(c, ORDER)
    og_s[...] = og[...].astype(F32) * gain_e

    for copy in pk_in:
        arrive(copy)
    totals = jnp.concatenate([pk[k // SIDE, k % SIDE, 0:1, :] for k in range(16)], axis=0)
    low16 = (iota((16, 16), 0) >= iota((16, 16), 1)).astype(F32)
    t_cum = jnp.dot(low16, totals, precision=HIGH, preferred_element_type=F32)
    t_e = jnp.dot(t_cum[:, :16], spread16, precision=HIGH, preferred_element_type=F32)
    for half in range(2):
        f0, s0 = first[half], second[half]
        parent = jnp.concatenate([(pk[s, f0] if half == 0 else pk[f0, s])[4:8] for s in range(SIDE)], axis=0)
        onehot = (parent[:, 32:48] == iota((16, 16), 1).astype(F32)).astype(F32)
        lo = half * HALF
        t_half = t_e[:, lo : lo + HALF]
        t_par = jnp.dot(onehot, t_half, precision=HIGH, preferred_element_type=F32)
        p_col = parent[:, 32:33]
        for f in range(SIDE):
            j = at(half, f, s0)
            pick = (iota((16, HALF), 0) == j).astype(F32)
            t_j = jnp.sum(t_half * pick, axis=0, keepdims=True)
            w = jnp.where(p_col >= j.astype(F32), jnp.exp(jnp.minimum(t_par - t_j, 0.0)), 0.0)
            for s in range(SIDE):
                wt[half, f, s, 0:4] = w[4 * s : 4 * s + 4]
    stats = pk[0, 0]
    for k in range(1, 16):
        stats = stats + pk[k // SIDE, k % SIDE]
    floor_count = jnp.maximum(stats[:, 64:65], 1.0)
    mean = stats[:, 65:66] / floor_count
    spread = jnp.sqrt(stats[:, 66:67] / floor_count - mean * mean + 1.0)
    mean_row = jnp.sum(table * mean, axis=0, keepdims=True)
    spread_row = jnp.sum(table * spread, axis=0, keepdims=True)
    adv_row = (returns - mean_row) / spread_row

    def send_along(buf, s_sem, r_sem, half, c, distances):
        copies = {}
        s0 = second[half]
        for r in distances:
            copies[r] = send(
                buf.at[half, c, s0],
                buf.at[half, c, s0],
                s_sem.at[half, c, r],
                r_sem.at[half, c, r],
                {"seq": at(half, first[half], (s0 + r) % SIDE)},
            )
        return copies

    for half in range(2):
        for copy in c_in[half]:
            arrive(copy)
    y_in = [[], []]
    for c in range(NCH):
        for half in range(2):
            f0, s0 = first[half], second[half]
            cs = slice(c * CW, (c + 1) * CW)
            for n, r in enumerate((0, 1, 3, 2)):
                f = (f0 + r) % SIDE
                if r:
                    arrive(u_in[half][c][(SIDE - r) % SIDE])
                u = ug[half, c, f]
                copies = {}
                for q in (2, 1, 3, 0):
                    s = (s0 + q) % SIDE
                    w = rows_to_tokens(wt[half, f, s, :, cs], CW)
                    part = mm(cg[half, s], u) * w
                    if n:
                        part = part + acc[q]
                    if n < 3:
                        acc[q] = part
                    elif q:
                        yp[half, c, q] = part.astype(BF16)
                        copies[q] = send(
                            yp.at[half, c, q],
                            yr.at[half, c, q],
                            y_ss.at[half, c, q],
                            y_rs.at[half, c, q],
                            {"seq": at(half, f0, s)},
                        )
                    else:
                        lo = half * HALF + c * CW
                        y_s[:, lo : lo + CW] = y_s[:, lo : lo + CW] + part * lift_e[:, lo : lo + CW]
            y_in[half].append(copies)

    p_in, q_in = [[], []], [[], []]
    for c in range(EARLY):
        for half in range(2):
            lo = half * HALF + c * CW
            ws = slice(lo, lo + CW)
            s0 = second[half]
            pg[half, c, s0] = (og_s[:, ws] * sz_s[:, ws] * lift_e[:, ws]).astype(BF16)

    for half in range(2):
        for s in range(SIDE):
            ct[half, s] = cg[half, s].astype(F32).T.astype(BF16)

    sq = jnp.zeros((BLOCK, 128), F32)
    al = jnp.zeros((BLOCK, 128), F32)
    for c in range(NCH):
        for half in range(2):
            lo = half * HALF + c * CW
            ws = slice(lo, lo + CW)
            got = None
            for q in (1, 3, 2):
                arrive(y_in[half][c][q])
                v = yr[half, c, q].astype(F32)
                got = v if got is None else got + v
            gated = (y_s[:, ws] + got * lift_e[:, ws]) * sz_s[:, ws]
            gated_s[:, ws] = gated
            if c < EARLY:
                qg[half, c, second[half]] = (gated * sz_s[:, ws] * lift_e[:, ws]).astype(BF16)
            squares = gated * gated
            inner = og_s[:, ws] * gated
            for k in range(CW // 128):
                sq = sq + squares[:, 128 * k : 128 * k + 128]
                al = al + inner[:, 128 * k : 128 * k + 128]
    sq_row = jnp.sum(sq.T, axis=0, keepdims=True)
    al_row = jnp.sum(al.T, axis=0, keepdims=True)
    ar[head] = jnp.where(sub == 0, sq_row, jnp.where(sub == 1, al_row, 0.0))
    ar_in = [
        send(ar.at[head], ar.at[head], ar_s.at[r], ar_r.at[r], {"head": (head + r) % 8}) for r in (4, 3, 5, 2, 6, 7, 1)
    ]
    for c in range(EARLY):
        for half in range(2):
            q_in[half].append(send_along(qg, qg_s, qg_r, half, c, (2,)))
            p_in[half].append(send_along(pg, pg_s, pg_r, half, c, (2,)))
    for copy in ar_in:
        arrive(copy)
    sums = ar[0]
    for k in range(1, 8):
        sums = sums + ar[k]
    scale = lax.rsqrt(sums[0:1] / (HEADS * HEAD_DIM) + EPSILON)
    along = adv_row * sums[1:2]
    kappa = scale * scale * scale * along / (HEADS * HEAD_DIM)
    sub128 = iota((128, 128), 0)
    rows = jnp.where(sub128 == 0, scale, jnp.where(sub128 == 1, scale * adv_row, jnp.where(sub128 == 2, kappa, 0.0)))
    sg[0, yi] = rows[0:8]
    sg[1, xi] = rows[0:8]
    s_in = [{}, {}]
    for r in (2,):
        for half in range(2):
            s0 = second[half]
            s_in[half][r] = send(
                sg.at[half, s0],
                sg.at[half, s0],
                sg_s.at[half, r],
                sg_r.at[half, r],
                {"seq": at(half, first[half], (s0 + r) % SIDE)},
            )
    cols = rows.T
    scale_c, push_c, kappa_c = cols[:, 0:1], cols[:, 1:2], cols[:, 2:3]

    d_in = [[], []]
    for c in range(NCH):
        for half in range(2):
            lo = half * HALF + c * CW
            ws = slice(lo, lo + CW)
            dy = (push_c * og_s[:, ws] - kappa_c * gated_s[:, ws]) * sz_s[:, ws]
            dy_s[:, ws] = dy
            f0, s0 = first[half], second[half]
            dg[half, c, s0] = (dy * lift_e[:, ws]).astype(BF16)
            d_in[half].append(send_along(dg, d_s, d_r, half, c, (1, 3) if c < EARLY else ORDER))

    scores_t = smat[...].astype(F32).T.astype(BF16)
    for c in range(NCH):
        for half in range(2):
            lo = half * HALF + c * CW
            ws = slice(lo, lo + CW)
            back = mm(scores_t, dg[half, c, second[half]]) * einv_e[:, ws] + skip_e[:, ws] * dy_s[:, ws]
            grad_o[:, ws] = back.astype(BF16)
    out_o[...] = (gated_s[...] * scale_c * gain_e).astype(BF16)

    g_in = [[], []]
    for c in range(NCH):
        for half in range(2):
            f0, s0 = first[half], second[half]
            cs = slice(c * CW, (c + 1) * CW)
            for n, r in enumerate((0, 2, 1, 3) if c < EARLY else (0, 1, 3, 2)):
                s = (s0 + r) % SIDE
                back = (SIDE - r) % SIDE
                if r == 2 and c < EARLY:
                    if c == 0:
                        arrive(s_in[half][back])
                        sg_c[half] = jnp.concatenate([sg[half, s], jnp.zeros((120, 128), F32)], axis=0).T
                    arrive(p_in[half][c][back])
                    arrive(q_in[half][c][back])
                    d = sg_c[half, :, 1:2] * pg[half, c, s].astype(F32)
                    d = d - sg_c[half, :, 2:3] * qg[half, c, s].astype(F32)
                else:
                    if r:
                        arrive(d_in[half][c][back])
                    d = dg[half, c, s].astype(F32)
                copies = {}
                for q in (2, 1, 3, 0):
                    f = (f0 + q) % SIDE
                    w = rows_to_tokens(wt[half, f, s, :, cs], CW)
                    part = mm(ct[half, s], (d * w).astype(BF16))
                    if n:
                        part = part + acc[q]
                    if n < 3 or q == 0:
                        acc[q if n < 3 else 4 + half * NCH + c] = part
                    else:
                        gp[half, c, q] = part.astype(BF16)
                        copies[q] = send(
                            gp.at[half, c, q],
                            gr.at[half, c, q],
                            g_s.at[half, c, q],
                            g_r.at[half, c, q],
                            {"seq": at(half, f, s0)},
                        )
            g_in[half].append(copies)

    p_b = pb[...]
    for c in range(NCH):
        for half in range(2):
            lo = half * HALF + c * CW
            ws = slice(lo, lo + CW)
            g = acc[4 + half * NCH + c]
            for q in (1, 3, 2):
                arrive(g_in[half][c][q])
                g = g + gr[half, c, q].astype(F32)
            prompt_o[:, ws] = mm(p_b, g.astype(BF16)) * tail_e[:, ws]

    for copy in sent:
        copy.wait_send()


PIECES = 4


def hand_over(a, b, c, a_out, b_out, c_out):
    a_out[...] = a[...]
    b_out[...] = b[...]
    c_out[...] = c[...]


def local(
    prompt_x, prompt_b, prompt_dt, branch_x, branch_b, branch_c, branch_z, branch_dt,
    a_rate, d_skip, norm_gain, branch_parent, group_ids, returns, out_grad,
):
    vm = pl.BlockSpec(memory_space=pltpu.VMEM)
    dma = pltpu.SemaphoreType.DMA
    V = pltpu.VMEM
    results = pl.pallas_call(
        kernel,
        out_shape=(
            jax.ShapeDtypeStruct((BLOCK, CH), BF16),
            jax.ShapeDtypeStruct((BLOCK, CH), BF16),
            jax.ShapeDtypeStruct((BLOCK, CH), F32),
        ),
        in_specs=[pl.BlockSpec(memory_space=pltpu.HBM)] * 15,
        out_specs=(vm, vm, vm),
        scratch_shapes=[
            V((BLOCK, CH), BF16), V((BLOCK, STATE), BF16), V((LOCAL_HEADS, BLOCK), F32),
            V((BLOCK, CH), BF16), V((BLOCK, STATE), BF16), V((BLOCK, STATE), BF16),
            V((BLOCK, CH), BF16), V((LOCAL_HEADS, BLOCK), F32),
            V((1, LOCAL_HEADS), F32), V((1, LOCAL_HEADS), F32), V((1, CH), F32),
            pltpu.SMEM((NB,), jnp.int32), V((1, BLOCK), jnp.int32), V((1, BLOCK), F32),
            V((BLOCK, CH), BF16),
            dma((15,)),
            V((SIDE, SIDE, 8, 128), F32),
            V((8, 8, 128), F32),
            V((2, NCH, SIDE, STATE, CW), BF16),
            V((2, SIDE, BLOCK, STATE), BF16),
            V((2, SIDE, STATE, BLOCK), BF16),
            V((2, NCH, SIDE, BLOCK, CW), BF16),
            V((2, NCH, SIDE, BLOCK, CW), BF16),
            V((2, NCH, SIDE, BLOCK, CW), BF16),
            V((2, NCH, SIDE, STATE, CW), BF16),
            V((2, NCH, SIDE, STATE, CW), BF16),
            V((4 + 2 * NCH, BLOCK, CW), F32),
            V((2, SIDE, SIDE, 8, HALF), F32),
            V((BLOCK, CH), F32),
            V((BLOCK, CH), F32),
            V((BLOCK, CH), F32),
            V((BLOCK, BLOCK), BF16),
            V((BLOCK, CH), F32),
            V((BLOCK, CH), F32),
            V((BLOCK, CH), F32),
            V((BLOCK, CH), F32),
            V((BLOCK, CH), F32),
            V((2, EARLY, SIDE, BLOCK, CW), BF16),
            V((2, EARLY, SIDE, BLOCK, CW), BF16),
            V((2, SIDE, 8, 128), F32),
            V((2, BLOCK, 128), F32),
            dma((2, EARLY, SIDE)), dma((2, EARLY, SIDE)),
            dma((2, EARLY, SIDE)), dma((2, EARLY, SIDE)),
            dma((2, SIDE)), dma((2, SIDE)),
            dma((2, SIDE)), dma((2, SIDE)), dma((8,)), dma((8,)),
            dma((2, NCH, SIDE)), dma((2, NCH, SIDE)),
            dma((2, SIDE)), dma((2, SIDE)),
            dma((2, NCH, SIDE)), dma((2, NCH, SIDE)),
            dma((2, NCH, SIDE)), dma((2, NCH, SIDE)),
            dma((2, NCH, SIDE)), dma((2, NCH, SIDE)),
        ],
        compiler_params=pltpu.CompilerParams(
            collective_id=0, has_side_effects=True, vmem_limit_bytes=40 * 2**20
        ),
    )(*(pltpu.with_memory_space_constraint(v, pltpu.HBM) for v in (
        prompt_x, prompt_b, prompt_dt, branch_x, branch_b, branch_c, branch_z, branch_dt,
        a_rate.reshape(1, -1), d_skip.reshape(1, -1), norm_gain.reshape(1, -1), branch_parent,
        group_ids.reshape(1, -1), returns.reshape(1, -1), out_grad,
    )))
    hbm = pl.BlockSpec(memory_space=pltpu.HBM)
    return pl.pallas_call(
        hand_over,
        out_shape=tuple(jax.ShapeDtypeStruct(r.shape, r.dtype) for r in results),
        in_specs=[vm] * 3,
        out_specs=(vm,) * 3,
        compiler_params=pltpu.CompilerParams(vmem_limit_bytes=16 * 2**20),
    )(*results)


def solution(mesh):
    rows = P(("parts", "seq"), "head")
    steps = P("head", ("parts", "seq"))
    heads = P("head")
    tokens = P(("parts", "seq"))
    return jax.shard_map(
        local,
        mesh=mesh,
        in_specs=(
            rows, rows, steps, rows, rows, rows, rows, steps,
            heads, heads, heads, tokens, tokens, tokens, rows,
        ),
        out_specs=(rows, rows, rows),
        check_vma=False,
    )
```

```python
import functools

import jax
import jax.numpy as jnp
from jax import lax
from jax.experimental import pallas as pl
from jax.experimental.pallas import tpu as pltpu
from jax.sharding import PartitionSpec as P

HEADS = 128
HEAD_DIM = 64
STATE = 128
BLOCK = 128
SEG = 32
NB = 4
EPSILON = 1e-05
SIDE = 4
LOCAL_HEADS = 16
CH = 1024
HALF = 512
NCH = 2
EARLY = 1
CW = HALF // NCH
MESH_ID = pl.DeviceIdType.MESH
F32 = jnp.float32
BF16 = jnp.bfloat16
HIGH = lax.Precision.HIGHEST


def iota(shape, dim):
    return lax.broadcasted_iota(jnp.int32, shape, dim)


def column(row, n):
    eye = iota((n, n), 0) == iota((n, n), 1)
    return jnp.sum(jnp.where(eye, jnp.broadcast_to(row, (n, n)), 0.0), axis=1, keepdims=True)


def split(v):
    high = v.astype(BF16).astype(F32)
    return high, v - high


def mm(a, b):
    return jnp.dot(a, b, preferred_element_type=F32)


def rows_to_tokens(w, width):
    return jnp.concatenate([jnp.broadcast_to(w[b : b + 1], (SEG, width)) for b in range(NB)], axis=0)


def kernel(
    px_h, pb_h, pdt_h, bx_h, bb_h, bc_h, bz_h, bdt_h, rate_h, skip_h, gain_h, par_h, gid_h, ret_h, og_h,
    out_o, grad_o, prompt_o,
    px, pb, pdt, bx, bb, bc, bz, bdt, rate, skip, gain, par, gid, ret, og, in_sem,
    pk, ar, ug, cg, ct, yp, yr, dg, gp, gr, acc, wt, tail_e, lift_e, einv_e, smat, y_s, gated_s, sz_s, dy_s, og_s, pg, qg, sg, sg_c,
    pg_s, pg_r, qg_s, qg_r, sg_s, sg_r,
    pk_s, pk_r, ar_s, ar_r, u_s, u_r, c_s, c_r, y_ss, y_rs, d_s, d_r, g_s, g_r,
):
    seq = lax.axis_index("seq")
    head = lax.axis_index("head")
    yi, xi = seq // SIDE, seq % SIDE

    loads = {}
    for n, (name, src, dst) in enumerate((
        ("pdt", pdt_h, pdt), ("rate", rate_h, rate), ("px", px_h, px), ("pb", pb_h, pb), ("bdt", bdt_h, bdt),
        ("par", par_h, par), ("gid", gid_h, gid), ("ret", ret_h, ret), ("bc", bc_h, bc), ("skip", skip_h, skip),
        ("bb", bb_h, bb), ("bx", bx_h, bx), ("bz", bz_h, bz), ("gain", gain_h, gain), ("og", og_h, og),
    )):
        loads[name] = pltpu.make_async_copy(src, dst, in_sem.at[n])
        loads[name].start()

    def loaded(*names):
        for name in names:
            loads[name].wait()

    barrier = pltpu.get_barrier_semaphore()
    for r in range(1, 8):
        pl.semaphore_signal(barrier, inc=1, device_id={"head": (head + r) % 8}, device_id_type=MESH_ID)
    for r in range(1, SIDE):
        pl.semaphore_signal(
            barrier, inc=1, device_id={"seq": yi * SIDE + (xi + r) % SIDE}, device_id_type=MESH_ID
        )
        pl.semaphore_signal(
            barrier, inc=1, device_id={"seq": (yi + r) % SIDE * SIDE + xi}, device_id_type=MESH_ID
        )

    first = (xi, yi)
    second = (yi, xi)

    def at(half, f, s):
        return s * SIDE + f if half == 0 else f * SIDE + s

    def send(src, dst, s_sem, r_sem, device):
        copy = pltpu.make_async_remote_copy(
            src_ref=src, dst_ref=dst, send_sem=s_sem, recv_sem=r_sem, device_id=device, device_id_type=MESH_ID
        )
        copy.start()
        sent.append(copy)
        return copy

    sent = []

    def arrive(copy):
        copy.wait_recv()

    loaded("pdt", "rate", "bdt")
    rate_c = column(rate[...], LOCAL_HEADS)
    upto = (iota((BLOCK, BLOCK), 0) <= iota((BLOCK, BLOCK), 1)).astype(F32)
    same = (iota((BLOCK, BLOCK), 0) // SEG) == (iota((BLOCK, BLOCK), 1) // SEG)
    upto_seg = jnp.where(same, upto, 0.0)
    p_dt = pdt[...]
    running = jnp.dot(p_dt * (-rate_c), upto, precision=HIGH, preferred_element_type=F32)
    total = running[:, BLOCK - 1 :]
    tails = jnp.exp(total - running) * p_dt
    b_dt = bdt[...]
    cum = jnp.dot(b_dt * (-rate_c), upto_seg, precision=HIGH, preferred_element_type=F32)
    lift = jnp.exp(cum)
    einv = jnp.exp(-cum) * b_dt

    stack = jnp.concatenate(
        [*split(tails), *split(lift), *split(einv), jnp.zeros((32, BLOCK), F32)], axis=0
    )
    stack_t = stack.T.astype(BF16)
    spread32 = ((iota((32, CH), 0) & 15) == (iota((32, CH), 1) >> 6)).astype(BF16)
    spread16 = ((iota((16, CH), 0)) == (iota((16, CH), 1) >> 6)).astype(F32)
    te = mm(stack_t[:, 0:32], spread32)
    tail_e[...] = te
    loaded("px", "pb")
    xw = (px[...].astype(F32) * te).astype(BF16)
    pb_t = pb[...].astype(F32).T.astype(BF16)
    for half in range(2):
        for c in range(NCH):
            lo = half * HALF + c * CW
            ug[half, c, first[half]] = mm(pb_t, xw[:, lo : lo + CW]).astype(BF16)

    loaded("par", "gid", "ret", "bc")
    sub = iota((8, 128), 0)
    lane = iota((8, 128), 1)
    eye16 = iota((16, 128), 0) == iota((16, 128), 1)
    total_row = jnp.sum(jnp.where(eye16, jnp.broadcast_to(total, (16, 128)), 0.0), axis=0, keepdims=True)
    parents = jnp.zeros((8, 128), F32)
    for b in range(NB):
        parents = jnp.where(sub == 4 + b, par[b].astype(F32), parents)
    table = (sub == jnp.broadcast_to(gid[...], (8, 128))).astype(F32)
    returns = ret[...]
    g_count = jnp.sum(table, axis=1, keepdims=True)
    g_sum = jnp.sum(table * returns, axis=1, keepdims=True)
    g_sq = jnp.sum(table * (returns * returns), axis=1, keepdims=True)
    tile = jnp.where(sub == 0, jnp.broadcast_to(total_row, (8, 128)), 0.0)
    tile = jnp.where((lane >= 32) & (lane < 48), parents, tile)
    for n, value in enumerate((g_count, g_sum, g_sq)):
        tile = jnp.where(lane == 64 + n, value, tile)
    pk[yi, xi] = tile
    c_own = bc[...]
    for half in range(2):
        cg[half, second[half]] = c_own

    pl.semaphore_wait(barrier, 13)

    pk_in, c_in, u_in = [], [[], []], [[], []]
    for r in (2, 1, 3):
        peer = yi * SIDE + (xi + r) % SIDE
        pk_in.append(send(pk.at[yi, xi], pk.at[yi, xi], pk_s.at[0, r], pk_r.at[0, r], {"seq": peer}))
    ORDER = (1, 3, 2)
    for half in range(2):
        s = second[half]
        for r in ORDER:
            peer = at(half, first[half], (s + r) % SIDE)
            c_in[half].append(
                send(cg.at[half, s], cg.at[half, s], c_s.at[half, r], c_r.at[half, r], {"seq": peer})
            )
    def send_updates(c, distances):
        for half in range(2):
            f = first[half]
            if len(u_in[half]) == c:
                u_in[half].append({})
            copies = u_in[half][c]
            for r in distances:
                peer = at(half, (f + r) % SIDE, second[half])
                copies[r] = send(
                    ug.at[half, c, f], ug.at[half, c, f], u_s.at[half, c, r], u_r.at[half, c, r], {"seq": peer}
                )

    send_updates(0, (1, 3))

    loaded("skip", "bb", "bx", "bz", "gain", "og")
    lift_e[...] = mm(stack_t[:, 32:64], spread32)
    einv_e[...] = mm(stack_t[:, 64:96], spread32)
    skip_e = jnp.sum(column(skip[...], LOCAL_HEADS) * spread16, axis=0, keepdims=True)
    gain_e = gain[...]
    scores = lax.dot_general(c_own, bb[...], (((1,), (1,)), ((), ())), preferred_element_type=F32)
    lower = upto_seg.T
    scores = (scores * lower).astype(BF16)
    smat[...] = scores
    x_own = bx[...].astype(F32)
    inner = mm(scores, (x_own * einv_e[...]).astype(BF16))
    y_s[...] = inner * lift_e[...] + skip_e * x_own
    z = bz[...].astype(F32)
    sz_s[...] = z / (1.0 + jnp.exp(-z))

    for copy in pk_in:
        arrive(copy)
    pk_in = []
    for r in (2, 1, 3):
        peer = (yi + r) % SIDE * SIDE + xi
        pk_in.append(send(pk.at[yi], pk.at[yi], pk_s.at[1, r], pk_r.at[1, r], {"seq": peer}))
    send_updates(0, (2,))
    for c in range(1, NCH):
        send_updates(c, ORDER)
    og_s[...] = og[...].astype(F32) * gain_e

    for copy in pk_in:
        arrive(copy)
    totals = jnp.concatenate([pk[k // SIDE, k % SIDE, 0:1, :] for k in range(16)], axis=0)
    low16 = (iota((16, 16), 0) >= iota((16, 16), 1)).astype(F32)
    t_cum = jnp.dot(low16, totals, precision=HIGH, preferred_element_type=F32)
    t_e = jnp.dot(t_cum[:, :16], spread16, precision=HIGH, preferred_element_type=F32)
    for half in range(2):
        f0, s0 = first[half], second[half]
        parent = jnp.concatenate([(pk[s, f0] if half == 0 else pk[f0, s])[4:8] for s in range(SIDE)], axis=0)
        onehot = (parent[:, 32:48] == iota((16, 16), 1).astype(F32)).astype(F32)
        lo = half * HALF
        t_half = t_e[:, lo : lo + HALF]
        t_par = jnp.dot(onehot, t_half, precision=HIGH, preferred_element_type=F32)
        p_col = parent[:, 32:33]
        for f in range(SIDE):
            j = at(half, f, s0)
            pick = (iota((16, HALF), 0) == j).astype(F32)
            t_j = jnp.sum(t_half * pick, axis=0, keepdims=True)
            w = jnp.where(p_col >= j.astype(F32), jnp.exp(jnp.minimum(t_par - t_j, 0.0)), 0.0)
            for s in range(SIDE):
                wt[half, f, s, 0:4] = w[4 * s : 4 * s + 4]
    stats = pk[0, 0]
    for k in range(1, 16):
        stats = stats + pk[k // SIDE, k % SIDE]
    floor_count = jnp.maximum(stats[:, 64:65], 1.0)
    mean = stats[:, 65:66] / floor_count
    spread = jnp.sqrt(stats[:, 66:67] / floor_count - mean * mean + 1.0)
    mean_row = jnp.sum(table * mean, axis=0, keepdims=True)
    spread_row = jnp.sum(table * spread, axis=0, keepdims=True)
    adv_row = (returns - mean_row) / spread_row

    def send_along(buf, s_sem, r_sem, half, c, distances):
        copies = {}
        s0 = second[half]
        for r in distances:
            copies[r] = send(
                buf.at[half, c, s0],
                buf.at[half, c, s0],
                s_sem.at[half, c, r],
                r_sem.at[half, c, r],
                {"seq": at(half, first[half], (s0 + r) % SIDE)},
            )
        return copies

    for half in range(2):
        for copy in c_in[half]:
            arrive(copy)
    y_in = [[], []]
    for c in range(NCH):
        for half in range(2):
            f0, s0 = first[half], second[half]
            cs = slice(c * CW, (c + 1) * CW)
            for n, r in enumerate((0, 1, 3, 2)):
                f = (f0 + r) % SIDE
                if r:
                    arrive(u_in[half][c][(SIDE - r) % SIDE])
                u = ug[half, c, f]
                copies = {}
                for q in (2, 1, 3, 0):
                    s = (s0 + q) % SIDE
                    w = rows_to_tokens(wt[half, f, s, :, cs], CW)
                    part = mm(cg[half, s], u) * w
                    if n:
                        part = part + acc[q]
                    if n < 3:
                        acc[q] = part
                    elif q:
                        yp[half, c, q] = part.astype(BF16)
                        copies[q] = send(
                            yp.at[half, c, q],
                            yr.at[half, c, q],
                            y_ss.at[half, c, q],
                            y_rs.at[half, c, q],
                            {"seq": at(half, f0, s)},
                        )
                    else:
                        lo = half * HALF + c * CW
                        y_s[:, lo : lo + CW] = y_s[:, lo : lo + CW] + part * lift_e[:, lo : lo + CW]
            y_in[half].append(copies)

    p_in, q_in = [[], []], [[], []]
    for c in range(EARLY):
        for half in range(2):
            lo = half * HALF + c * CW
            ws = slice(lo, lo + CW)
            s0 = second[half]
            pg[half, c, s0] = (og_s[:, ws] * sz_s[:, ws] * lift_e[:, ws]).astype(BF16)

    for half in range(2):
        for s in range(SIDE):
            ct[half, s] = cg[half, s].astype(F32).T.astype(BF16)

    sq = jnp.zeros((BLOCK, 128), F32)
    al = jnp.zeros((BLOCK, 128), F32)
    for c in range(NCH):
        for half in range(2):
            lo = half * HALF + c * CW
            ws = slice(lo, lo + CW)
            got = None
            for q in (1, 3, 2):
                arrive(y_in[half][c][q])
                v = yr[half, c, q].astype(F32)
                got = v if got is None else got + v
            gated = (y_s[:, ws] + got * lift_e[:, ws]) * sz_s[:, ws]
            gated_s[:, ws] = gated
            if c < EARLY:
                qg[half, c, second[half]] = (gated * sz_s[:, ws] * lift_e[:, ws]).astype(BF16)
            squares = gated * gated
            inner = og_s[:, ws] * gated
            for k in range(CW // 128):
                sq = sq + squares[:, 128 * k : 128 * k + 128]
                al = al + inner[:, 128 * k : 128 * k + 128]
    sq_row = jnp.sum(sq.T, axis=0, keepdims=True)
    al_row = jnp.sum(al.T, axis=0, keepdims=True)
    ar[head] = jnp.where(sub == 0, sq_row, jnp.where(sub == 1, al_row, 0.0))
    ar_in = [
        send(ar.at[head], ar.at[head], ar_s.at[r], ar_r.at[r], {"head": (head + r) % 8}) for r in (4, 3, 5, 2, 6, 7, 1)
    ]
    for c in range(EARLY):
        for half in range(2):
            q_in[half].append(send_along(qg, qg_s, qg_r, half, c, (2,)))
            p_in[half].append(send_along(pg, pg_s, pg_r, half, c, (2,)))
    for copy in ar_in:
        arrive(copy)
    sums = ar[0]
    for k in range(1, 8):
        sums = sums + ar[k]
    scale = lax.rsqrt(sums[0:1] / (HEADS * HEAD_DIM) + EPSILON)
    along = adv_row * sums[1:2]
    kappa = scale * scale * scale * along / (HEADS * HEAD_DIM)
    sub128 = iota((128, 128), 0)
    rows = jnp.where(sub128 == 0, scale, jnp.where(sub128 == 1, scale * adv_row, jnp.where(sub128 == 2, kappa, 0.0)))
    sg[0, yi] = rows[0:8]
    sg[1, xi] = rows[0:8]
    s_in = [{}, {}]
    for r in (2,):
        for half in range(2):
            s0 = second[half]
            s_in[half][r] = send(
                sg.at[half, s0],
                sg.at[half, s0],
                sg_s.at[half, r],
                sg_r.at[half, r],
                {"seq": at(half, first[half], (s0 + r) % SIDE)},
            )
    cols = rows.T
    scale_c, push_c, kappa_c = cols[:, 0:1], cols[:, 1:2], cols[:, 2:3]

    d_in = [[], []]
    for c in range(NCH):
        for half in range(2):
            lo = half * HALF + c * CW
            ws = slice(lo, lo + CW)
            dy = (push_c * og_s[:, ws] - kappa_c * gated_s[:, ws]) * sz_s[:, ws]
            dy_s[:, ws] = dy
            f0, s0 = first[half], second[half]
            dg[half, c, s0] = (dy * lift_e[:, ws]).astype(BF16)
            d_in[half].append(send_along(dg, d_s, d_r, half, c, (1, 3) if c < EARLY else ORDER))

    scores_t = smat[...].astype(F32).T.astype(BF16)
    for c in range(NCH):
        for half in range(2):
            lo = half * HALF + c * CW
            ws = slice(lo, lo + CW)
            back = mm(scores_t, dg[half, c, second[half]]) * einv_e[:, ws] + skip_e[:, ws] * dy_s[:, ws]
            grad_o[:, ws] = back.astype(BF16)
    out_o[...] = (gated_s[...] * scale_c * gain_e).astype(BF16)

    g_in = [[], []]
    for c in range(NCH):
        for half in range(2):
            f0, s0 = first[half], second[half]
            cs = slice(c * CW, (c + 1) * CW)
            for n, r in enumerate((0, 2, 1, 3) if c < EARLY else (0, 1, 3, 2)):
                s = (s0 + r) % SIDE
                back = (SIDE - r) % SIDE
                if r == 2 and c < EARLY:
                    if c == 0:
                        arrive(s_in[half][back])
                        sg_c[half] = jnp.concatenate([sg[half, s], jnp.zeros((120, 128), F32)], axis=0).T
                    arrive(p_in[half][c][back])
                    arrive(q_in[half][c][back])
                    d = sg_c[half, :, 1:2] * pg[half, c, s].astype(F32)
                    d = d - sg_c[half, :, 2:3] * qg[half, c, s].astype(F32)
                else:
                    if r:
                        arrive(d_in[half][c][back])
                    d = dg[half, c, s].astype(F32)
                copies = {}
                for q in (2, 1, 3, 0):
                    f = (f0 + q) % SIDE
                    w = rows_to_tokens(wt[half, f, s, :, cs], CW)
                    part = mm(ct[half, s], (d * w).astype(BF16))
                    if n:
                        part = part + acc[q]
                    if n < 3 or q == 0:
                        acc[q if n < 3 else 4 + half * NCH + c] = part
                    else:
                        gp[half, c, q] = part.astype(BF16)
                        copies[q] = send(
                            gp.at[half, c, q],
                            gr.at[half, c, q],
                            g_s.at[half, c, q],
                            g_r.at[half, c, q],
                            {"seq": at(half, f, s0)},
                        )
            g_in[half].append(copies)

    p_b = pb[...]
    for c in range(NCH):
        for half in range(2):
            lo = half * HALF + c * CW
            ws = slice(lo, lo + CW)
            g = acc[4 + half * NCH + c]
            for q in (1, 3, 2):
                arrive(g_in[half][c][q])
                g = g + gr[half, c, q].astype(F32)
            prompt_o[:, ws] = mm(p_b, g.astype(BF16)) * tail_e[:, ws]

    for copy in sent:
        copy.wait_send()


PIECES = 4


def hand_over(a, b, c, a_out, b_out, c_out, sem):
    copies = [
        pltpu.make_async_copy(src, dst, sem.at[n])
        for n, (src, dst) in enumerate(((c, c_out), (a, a_out), (b, b_out)))
    ]
    for copy in copies:
        copy.start()
    for copy in copies:
        copy.wait()


def local(
    prompt_x, prompt_b, prompt_dt, branch_x, branch_b, branch_c, branch_z, branch_dt,
    a_rate, d_skip, norm_gain, branch_parent, group_ids, returns, out_grad,
):
    vm = pl.BlockSpec(memory_space=pltpu.VMEM)
    dma = pltpu.SemaphoreType.DMA
    V = pltpu.VMEM
    results = pl.pallas_call(
        kernel,
        out_shape=(
            jax.ShapeDtypeStruct((BLOCK, CH), BF16),
            jax.ShapeDtypeStruct((BLOCK, CH), BF16),
            jax.ShapeDtypeStruct((BLOCK, CH), F32),
        ),
        in_specs=[pl.BlockSpec(memory_space=pltpu.HBM)] * 15,
        out_specs=(vm, vm, vm),
        scratch_shapes=[
            V((BLOCK, CH), BF16), V((BLOCK, STATE), BF16), V((LOCAL_HEADS, BLOCK), F32),
            V((BLOCK, CH), BF16), V((BLOCK, STATE), BF16), V((BLOCK, STATE), BF16),
            V((BLOCK, CH), BF16), V((LOCAL_HEADS, BLOCK), F32),
            V((1, LOCAL_HEADS), F32), V((1, LOCAL_HEADS), F32), V((1, CH), F32),
            pltpu.SMEM((NB,), jnp.int32), V((1, BLOCK), jnp.int32), V((1, BLOCK), F32),
            V((BLOCK, CH), BF16),
            dma((15,)),
            V((SIDE, SIDE, 8, 128), F32),
            V((8, 8, 128), F32),
            V((2, NCH, SIDE, STATE, CW), BF16),
            V((2, SIDE, BLOCK, STATE), BF16),
            V((2, SIDE, STATE, BLOCK), BF16),
            V((2, NCH, SIDE, BLOCK, CW), BF16),
            V((2, NCH, SIDE, BLOCK, CW), BF16),
            V((2, NCH, SIDE, BLOCK, CW), BF16),
            V((2, NCH, SIDE, STATE, CW), BF16),
            V((2, NCH, SIDE, STATE, CW), BF16),
            V((4 + 2 * NCH, BLOCK, CW), F32),
            V((2, SIDE, SIDE, 8, HALF), F32),
            V((BLOCK, CH), F32),
            V((BLOCK, CH), F32),
            V((BLOCK, CH), F32),
            V((BLOCK, BLOCK), BF16),
            V((BLOCK, CH), F32),
            V((BLOCK, CH), F32),
            V((BLOCK, CH), F32),
            V((BLOCK, CH), F32),
            V((BLOCK, CH), F32),
            V((2, EARLY, SIDE, BLOCK, CW), BF16),
            V((2, EARLY, SIDE, BLOCK, CW), BF16),
            V((2, SIDE, 8, 128), F32),
            V((2, BLOCK, 128), F32),
            dma((2, EARLY, SIDE)), dma((2, EARLY, SIDE)),
            dma((2, EARLY, SIDE)), dma((2, EARLY, SIDE)),
            dma((2, SIDE)), dma((2, SIDE)),
            dma((2, SIDE)), dma((2, SIDE)), dma((8,)), dma((8,)),
            dma((2, NCH, SIDE)), dma((2, NCH, SIDE)),
            dma((2, SIDE)), dma((2, SIDE)),
            dma((2, NCH, SIDE)), dma((2, NCH, SIDE)),
            dma((2, NCH, SIDE)), dma((2, NCH, SIDE)),
            dma((2, NCH, SIDE)), dma((2, NCH, SIDE)),
        ],
        compiler_params=pltpu.CompilerParams(
            collective_id=0, has_side_effects=True, vmem_limit_bytes=40 * 2**20
        ),
    )(*(pltpu.with_memory_space_constraint(v, pltpu.HBM) for v in (
        prompt_x, prompt_b, prompt_dt, branch_x, branch_b, branch_c, branch_z, branch_dt,
        a_rate.reshape(1, -1), d_skip.reshape(1, -1), norm_gain.reshape(1, -1), branch_parent,
        group_ids.reshape(1, -1), returns.reshape(1, -1), out_grad,
    )))
    hbm = pl.BlockSpec(memory_space=pltpu.HBM)
    return pl.pallas_call(
        hand_over,
        out_shape=tuple(jax.ShapeDtypeStruct(r.shape, r.dtype) for r in results),
        in_specs=[vm] * 3,
        out_specs=(hbm,) * 3,
        scratch_shapes=[dma((3,))],
        compiler_params=pltpu.CompilerParams(vmem_limit_bytes=16 * 2**20),
    )(*results)


def solution(mesh):
    rows = P(("parts", "seq"), "head")
    steps = P("head", ("parts", "seq"))
    heads = P("head")
    tokens = P(("parts", "seq"))
    return jax.shard_map(
        local,
        mesh=mesh,
        in_specs=(
            rows, rows, steps, rows, rows, rows, rows, steps,
            heads, heads, heads, tokens, tokens, tokens, rows,
        ),
        out_specs=(rows, rows, rows),
        check_vma=False,
    )
```

```python
import functools

import jax
import jax.numpy as jnp
from jax import lax
from jax.experimental import pallas as pl
from jax.experimental.pallas import tpu as pltpu
from jax.sharding import PartitionSpec as P

HEADS = 128
HEAD_DIM = 64
STATE = 128
BLOCK = 128
SEG = 32
NB = 4
EPSILON = 1e-05
SIDE = 4
LOCAL_HEADS = 16
CH = 1024
HALF = 512
NCH = 2
EARLY = 1
CW = HALF // NCH
MESH_ID = pl.DeviceIdType.MESH
F32 = jnp.float32
BF16 = jnp.bfloat16
HIGH = lax.Precision.HIGHEST


def iota(shape, dim):
    return lax.broadcasted_iota(jnp.int32, shape, dim)


def column(row, n):
    eye = iota((n, n), 0) == iota((n, n), 1)
    return jnp.sum(jnp.where(eye, jnp.broadcast_to(row, (n, n)), 0.0), axis=1, keepdims=True)


def split(v):
    high = v.astype(BF16).astype(F32)
    return high, v - high


def mm(a, b):
    return jnp.dot(a, b, preferred_element_type=F32)


def rows_to_tokens(w, width):
    return jnp.concatenate([jnp.broadcast_to(w[b : b + 1], (SEG, width)) for b in range(NB)], axis=0)


def kernel(
    px_h, pb_h, pdt_h, bx_h, bb_h, bc_h, bz_h, bdt_h, rate_h, skip_h, gain_h, par_h, gid_h, ret_h, og_h,
    out_o, grad_o, prompt_o,
    px, pb, pdt, bx, bb, bc, bz, bdt, rate, skip, gain, par, gid, ret, og, in_sem,
    pk, ar, ug, cg, ct, yp, yr, dg, gp, gr, acc, wt, tail_e, lift_e, einv_e, smat, y_s, gated_s, sz_s, dy_s, og_s, pg, qg, sg, sg_c,
    pg_s, pg_r, qg_s, qg_r, sg_s, sg_r,
    pk_s, pk_r, ar_s, ar_r, u_s, u_r, c_s, c_r, y_ss, y_rs, d_s, d_r, g_s, g_r,
):
    seq = lax.axis_index("seq")
    head = lax.axis_index("head")
    yi, xi = seq // SIDE, seq % SIDE

    loads = {}
    for n, (name, src, dst) in enumerate((
        ("pdt", pdt_h, pdt), ("rate", rate_h, rate), ("px", px_h, px), ("pb", pb_h, pb), ("bdt", bdt_h, bdt),
        ("par", par_h, par), ("gid", gid_h, gid), ("ret", ret_h, ret), ("bc", bc_h, bc), ("skip", skip_h, skip),
        ("bb", bb_h, bb), ("bx", bx_h, bx), ("bz", bz_h, bz), ("gain", gain_h, gain), ("og", og_h, og),
    )):
        loads[name] = pltpu.make_async_copy(src, dst, in_sem.at[n])
        loads[name].start()

    def loaded(*names):
        for name in names:
            loads[name].wait()

    barrier = pltpu.get_barrier_semaphore()
    for r in range(1, 8):
        pl.semaphore_signal(barrier, inc=1, device_id={"head": (head + r) % 8}, device_id_type=MESH_ID)
    for r in range(1, SIDE):
        pl.semaphore_signal(
            barrier, inc=1, device_id={"seq": yi * SIDE + (xi + r) % SIDE}, device_id_type=MESH_ID
        )
        pl.semaphore_signal(
            barrier, inc=1, device_id={"seq": (yi + r) % SIDE * SIDE + xi}, device_id_type=MESH_ID
        )

    first = (xi, yi)
    second = (yi, xi)

    def at(half, f, s):
        return s * SIDE + f if half == 0 else f * SIDE + s

    def send(src, dst, s_sem, r_sem, device):
        copy = pltpu.make_async_remote_copy(
            src_ref=src, dst_ref=dst, send_sem=s_sem, recv_sem=r_sem, device_id=device, device_id_type=MESH_ID
        )
        copy.start()
        sent.append(copy)
        return copy

    sent = []

    def arrive(copy):
        copy.wait_recv()

    loaded("pdt", "rate", "bdt")
    rate_c = column(rate[...], LOCAL_HEADS)
    upto = (iota((BLOCK, BLOCK), 0) <= iota((BLOCK, BLOCK), 1)).astype(F32)
    same = (iota((BLOCK, BLOCK), 0) // SEG) == (iota((BLOCK, BLOCK), 1) // SEG)
    upto_seg = jnp.where(same, upto, 0.0)
    p_dt = pdt[...]
    running = jnp.dot(p_dt * (-rate_c), upto, precision=HIGH, preferred_element_type=F32)
    total = running[:, BLOCK - 1 :]
    tails = jnp.exp(total - running) * p_dt
    b_dt = bdt[...]
    cum = jnp.dot(b_dt * (-rate_c), upto_seg, precision=HIGH, preferred_element_type=F32)
    lift = jnp.exp(cum)
    einv = jnp.exp(-cum) * b_dt

    stack = jnp.concatenate(
        [*split(tails), *split(lift), *split(einv), jnp.zeros((32, BLOCK), F32)], axis=0
    )
    stack_t = stack.T.astype(BF16)
    spread32 = ((iota((32, CH), 0) & 15) == (iota((32, CH), 1) >> 6)).astype(BF16)
    spread16 = ((iota((16, CH), 0)) == (iota((16, CH), 1) >> 6)).astype(F32)
    te = mm(stack_t[:, 0:32], spread32)
    tail_e[...] = te
    loaded("px", "pb")
    xw = (px[...].astype(F32) * te).astype(BF16)
    pb_t = pb[...].astype(F32).T.astype(BF16)
    for half in range(2):
        for c in range(NCH):
            lo = half * HALF + c * CW
            ug[half, c, first[half]] = mm(pb_t, xw[:, lo : lo + CW]).astype(BF16)

    loaded("par", "gid", "ret", "bc")
    sub = iota((8, 128), 0)
    lane = iota((8, 128), 1)
    eye16 = iota((16, 128), 0) == iota((16, 128), 1)
    total_row = jnp.sum(jnp.where(eye16, jnp.broadcast_to(total, (16, 128)), 0.0), axis=0, keepdims=True)
    parents = jnp.zeros((8, 128), F32)
    for b in range(NB):
        parents = jnp.where(sub == 4 + b, par[b].astype(F32), parents)
    table = (sub == jnp.broadcast_to(gid[...], (8, 128))).astype(F32)
    returns = ret[...]
    g_count = jnp.sum(table, axis=1, keepdims=True)
    g_sum = jnp.sum(table * returns, axis=1, keepdims=True)
    g_sq = jnp.sum(table * (returns * returns), axis=1, keepdims=True)
    tile = jnp.where(sub == 0, jnp.broadcast_to(total_row, (8, 128)), 0.0)
    tile = jnp.where((lane >= 32) & (lane < 48), parents, tile)
    for n, value in enumerate((g_count, g_sum, g_sq)):
        tile = jnp.where(lane == 64 + n, value, tile)
    pk[yi, xi] = tile
    c_own = bc[...]
    for half in range(2):
        cg[half, second[half]] = c_own

    pl.semaphore_wait(barrier, 13)

    pk_in, c_in, u_in = [], [[], []], [[], []]
    for r in (2, 1, 3):
        peer = yi * SIDE + (xi + r) % SIDE
        pk_in.append(send(pk.at[yi, xi], pk.at[yi, xi], pk_s.at[0, r], pk_r.at[0, r], {"seq": peer}))
    ORDER = (1, 3, 2)
    for half in range(2):
        s = second[half]
        for r in ORDER:
            peer = at(half, first[half], (s + r) % SIDE)
            c_in[half].append(
                send(cg.at[half, s], cg.at[half, s], c_s.at[half, r], c_r.at[half, r], {"seq": peer})
            )
    def send_updates(c, distances):
        for half in range(2):
            f = first[half]
            if len(u_in[half]) == c:
                u_in[half].append({})
            copies = u_in[half][c]
            for r in distances:
                peer = at(half, (f + r) % SIDE, second[half])
                copies[r] = send(
                    ug.at[half, c, f], ug.at[half, c, f], u_s.at[half, c, r], u_r.at[half, c, r], {"seq": peer}
                )

    send_updates(0, (1, 3))

    loaded("skip", "bb", "bx", "bz", "gain", "og")
    lift_e[...] = mm(stack_t[:, 32:64], spread32)
    einv_e[...] = mm(stack_t[:, 64:96], spread32)
    skip_e = jnp.sum(column(skip[...], LOCAL_HEADS) * spread16, axis=0, keepdims=True)
    gain_e = gain[...]
    scores = lax.dot_general(c_own, bb[...], (((1,), (1,)), ((), ())), preferred_element_type=F32)
    lower = upto_seg.T
    scores = (scores * lower).astype(BF16)
    smat[...] = scores
    x_own = bx[...].astype(F32)
    inner = mm(scores, (x_own * einv_e[...]).astype(BF16))
    y_s[...] = inner * lift_e[...] + skip_e * x_own
    z = bz[...].astype(F32)
    sz_s[...] = z / (1.0 + jnp.exp(-z))

    for copy in pk_in:
        arrive(copy)
    pk_in = []
    for r in (2, 1, 3):
        peer = (yi + r) % SIDE * SIDE + xi
        pk_in.append(send(pk.at[yi], pk.at[yi], pk_s.at[1, r], pk_r.at[1, r], {"seq": peer}))
    send_updates(0, (2,))
    for c in range(1, NCH):
        send_updates(c, ORDER)
    og_s[...] = og[...].astype(F32) * gain_e

    for copy in pk_in:
        arrive(copy)
    totals = jnp.concatenate([pk[k // SIDE, k % SIDE, 0:1, :] for k in range(16)], axis=0)
    low16 = (iota((16, 16), 0) >= iota((16, 16), 1)).astype(F32)
    t_cum = jnp.dot(low16, totals, precision=HIGH, preferred_element_type=F32)
    t_e = jnp.dot(t_cum[:, :16], spread16, precision=HIGH, preferred_element_type=F32)
    for half in range(2):
        f0, s0 = first[half], second[half]
        parent = jnp.concatenate([(pk[s, f0] if half == 0 else pk[f0, s])[4:8] for s in range(SIDE)], axis=0)
        onehot = (parent[:, 32:48] == iota((16, 16), 1).astype(F32)).astype(F32)
        lo = half * HALF
        t_half = t_e[:, lo : lo + HALF]
        t_par = jnp.dot(onehot, t_half, precision=HIGH, preferred_element_type=F32)
        p_col = parent[:, 32:33]
        for f in range(SIDE):
            j = at(half, f, s0)
            pick = (iota((16, HALF), 0) == j).astype(F32)
            t_j = jnp.sum(t_half * pick, axis=0, keepdims=True)
            w = jnp.where(p_col >= j.astype(F32), jnp.exp(jnp.minimum(t_par - t_j, 0.0)), 0.0)
            for s in range(SIDE):
                wt[half, f, s, 0:4] = w[4 * s : 4 * s + 4]
    stats = pk[0, 0]
    for k in range(1, 16):
        stats = stats + pk[k // SIDE, k % SIDE]
    floor_count = jnp.maximum(stats[:, 64:65], 1.0)
    mean = stats[:, 65:66] / floor_count
    spread = jnp.sqrt(stats[:, 66:67] / floor_count - mean * mean + 1.0)
    mean_row = jnp.sum(table * mean, axis=0, keepdims=True)
    spread_row = jnp.sum(table * spread, axis=0, keepdims=True)
    adv_row = (returns - mean_row) / spread_row

    def send_along(buf, s_sem, r_sem, half, c, distances):
        copies = {}
        s0 = second[half]
        for r in distances:
            copies[r] = send(
                buf.at[half, c, s0],
                buf.at[half, c, s0],
                s_sem.at[half, c, r],
                r_sem.at[half, c, r],
                {"seq": at(half, first[half], (s0 + r) % SIDE)},
            )
        return copies

    for half in range(2):
        for copy in c_in[half]:
            arrive(copy)
    y_in = [[], []]
    for c in range(NCH):
        for half in range(2):
            f0, s0 = first[half], second[half]
            cs = slice(c * CW, (c + 1) * CW)
            for n, r in enumerate((0, 1, 3, 2)):
                f = (f0 + r) % SIDE
                if r:
                    arrive(u_in[half][c][(SIDE - r) % SIDE])
                u = ug[half, c, f]
                copies = {}
                for q in (2, 1, 3, 0):
                    s = (s0 + q) % SIDE
                    w = rows_to_tokens(wt[half, f, s, :, cs], CW)
                    part = mm(cg[half, s], u) * w
                    if n:
                        part = part + acc[q]
                    if n < 3:
                        acc[q] = part
                    elif q:
                        yp[half, c, q] = part.astype(BF16)
                        copies[q] = send(
                            yp.at[half, c, q],
                            yr.at[half, c, q],
                            y_ss.at[half, c, q],
                            y_rs.at[half, c, q],
                            {"seq": at(half, f0, s)},
                        )
                    else:
                        lo = half * HALF + c * CW
                        y_s[:, lo : lo + CW] = y_s[:, lo : lo + CW] + part * lift_e[:, lo : lo + CW]
            y_in[half].append(copies)

    p_in, q_in = [[], []], [[], []]
    for c in range(EARLY):
        for half in range(2):
            lo = half * HALF + c * CW
            ws = slice(lo, lo + CW)
            s0 = second[half]
            pg[half, c, s0] = (og_s[:, ws] * sz_s[:, ws] * lift_e[:, ws]).astype(BF16)

    for half in range(2):
        for s in range(SIDE):
            ct[half, s] = cg[half, s].astype(F32).T.astype(BF16)

    sq = jnp.zeros((BLOCK, 128), F32)
    al = jnp.zeros((BLOCK, 128), F32)
    for c in range(NCH):
        for half in range(2):
            lo = half * HALF + c * CW
            ws = slice(lo, lo + CW)
            got = None
            for q in (1, 3, 2):
                arrive(y_in[half][c][q])
                v = yr[half, c, q].astype(F32)
                got = v if got is None else got + v
            gated = (y_s[:, ws] + got * lift_e[:, ws]) * sz_s[:, ws]
            gated_s[:, ws] = gated
            if c < EARLY:
                qg[half, c, second[half]] = (gated * sz_s[:, ws] * lift_e[:, ws]).astype(BF16)
            squares = gated * gated
            inner = og_s[:, ws] * gated
            for k in range(CW // 128):
                sq = sq + squares[:, 128 * k : 128 * k + 128]
                al = al + inner[:, 128 * k : 128 * k + 128]
    sq_row = jnp.sum(sq.T, axis=0, keepdims=True)
    al_row = jnp.sum(al.T, axis=0, keepdims=True)
    ar[head] = jnp.where(sub == 0, sq_row, jnp.where(sub == 1, al_row, 0.0))
    ar_in = [
        send(ar.at[head], ar.at[head], ar_s.at[r], ar_r.at[r], {"head": (head + r) % 8}) for r in (4, 5, 3, 6, 2, 7, 1)
    ]
    for c in range(EARLY):
        for half in range(2):
            q_in[half].append(send_along(qg, qg_s, qg_r, half, c, (2,)))
            p_in[half].append(send_along(pg, pg_s, pg_r, half, c, (2,)))
    for copy in ar_in:
        arrive(copy)
    sums = ar[0]
    for k in range(1, 8):
        sums = sums + ar[k]
    scale = lax.rsqrt(sums[0:1] / (HEADS * HEAD_DIM) + EPSILON)
    along = adv_row * sums[1:2]
    kappa = scale * scale * scale * along / (HEADS * HEAD_DIM)
    sub128 = iota((128, 128), 0)
    rows = jnp.where(sub128 == 0, scale, jnp.where(sub128 == 1, scale * adv_row, jnp.where(sub128 == 2, kappa, 0.0)))
    sg[0, yi] = rows[0:8]
    sg[1, xi] = rows[0:8]
    s_in = [{}, {}]
    for r in (2,):
        for half in range(2):
            s0 = second[half]
            s_in[half][r] = send(
                sg.at[half, s0],
                sg.at[half, s0],
                sg_s.at[half, r],
                sg_r.at[half, r],
                {"seq": at(half, first[half], (s0 + r) % SIDE)},
            )
    cols = rows.T
    scale_c, push_c, kappa_c = cols[:, 0:1], cols[:, 1:2], cols[:, 2:3]

    d_in = [[], []]
    for c in range(NCH):
        for half in range(2):
            lo = half * HALF + c * CW
            ws = slice(lo, lo + CW)
            dy = (push_c * og_s[:, ws] - kappa_c * gated_s[:, ws]) * sz_s[:, ws]
            dy_s[:, ws] = dy
            f0, s0 = first[half], second[half]
            dg[half, c, s0] = (dy * lift_e[:, ws]).astype(BF16)
            d_in[half].append(send_along(dg, d_s, d_r, half, c, (1, 3) if c < EARLY else (2, 1, 3)))

    scores_t = smat[...].astype(F32).T.astype(BF16)
    for c in range(NCH):
        for half in range(2):
            lo = half * HALF + c * CW
            ws = slice(lo, lo + CW)
            back = mm(scores_t, dg[half, c, second[half]]) * einv_e[:, ws] + skip_e[:, ws] * dy_s[:, ws]
            grad_o[:, ws] = back.astype(BF16)
    out_o[...] = (gated_s[...] * scale_c * gain_e).astype(BF16)

    g_in = [[], []]
    for c in range(NCH):
        for half in range(2):
            f0, s0 = first[half], second[half]
            cs = slice(c * CW, (c + 1) * CW)
            for n, r in enumerate((0, 2, 1, 3) if c < EARLY else (0, 1, 3, 2)):
                s = (s0 + r) % SIDE
                back = (SIDE - r) % SIDE
                if r == 2 and c < EARLY:
                    if c == 0:
                        arrive(s_in[half][back])
                        sg_c[half] = jnp.concatenate([sg[half, s], jnp.zeros((120, 128), F32)], axis=0).T
                    arrive(p_in[half][c][back])
                    arrive(q_in[half][c][back])
                    d = sg_c[half, :, 1:2] * pg[half, c, s].astype(F32)
                    d = d - sg_c[half, :, 2:3] * qg[half, c, s].astype(F32)
                else:
                    if r:
                        arrive(d_in[half][c][back])
                    d = dg[half, c, s].astype(F32)
                copies = {}
                for q in (2, 1, 3, 0):
                    f = (f0 + q) % SIDE
                    w = rows_to_tokens(wt[half, f, s, :, cs], CW)
                    part = mm(ct[half, s], (d * w).astype(BF16))
                    if n:
                        part = part + acc[q]
                    if n < 3 or q == 0:
                        acc[q if n < 3 else 4 + half * NCH + c] = part
                    else:
                        gp[half, c, q] = part.astype(BF16)
                        copies[q] = send(
                            gp.at[half, c, q],
                            gr.at[half, c, q],
                            g_s.at[half, c, q],
                            g_r.at[half, c, q],
                            {"seq": at(half, f, s0)},
                        )
            g_in[half].append(copies)

    p_b = pb[...]
    for c in range(NCH):
        for half in range(2):
            lo = half * HALF + c * CW
            ws = slice(lo, lo + CW)
            g = acc[4 + half * NCH + c]
            for q in (1, 3, 2):
                arrive(g_in[half][c][q])
                g = g + gr[half, c, q].astype(F32)
            prompt_o[:, ws] = mm(p_b, g.astype(BF16)) * tail_e[:, ws]

    for copy in sent:
        copy.wait_send()


PIECES = 4


def hand_over(a, b, c, a_out, b_out, c_out, sem):
    copies = [
        pltpu.make_async_copy(src, dst, sem.at[n])
        for n, (src, dst) in enumerate(((c, c_out), (a, a_out), (b, b_out)))
    ]
    for copy in copies:
        copy.start()
    for copy in copies:
        copy.wait()


def local(
    prompt_x, prompt_b, prompt_dt, branch_x, branch_b, branch_c, branch_z, branch_dt,
    a_rate, d_skip, norm_gain, branch_parent, group_ids, returns, out_grad,
):
    vm = pl.BlockSpec(memory_space=pltpu.VMEM)
    dma = pltpu.SemaphoreType.DMA
    V = pltpu.VMEM
    results = pl.pallas_call(
        kernel,
        out_shape=(
            jax.ShapeDtypeStruct((BLOCK, CH), BF16),
            jax.ShapeDtypeStruct((BLOCK, CH), BF16),
            jax.ShapeDtypeStruct((BLOCK, CH), F32),
        ),
        in_specs=[pl.BlockSpec(memory_space=pltpu.HBM)] * 15,
        out_specs=(vm, vm, vm),
        scratch_shapes=[
            V((BLOCK, CH), BF16), V((BLOCK, STATE), BF16), V((LOCAL_HEADS, BLOCK), F32),
            V((BLOCK, CH), BF16), V((BLOCK, STATE), BF16), V((BLOCK, STATE), BF16),
            V((BLOCK, CH), BF16), V((LOCAL_HEADS, BLOCK), F32),
            V((1, LOCAL_HEADS), F32), V((1, LOCAL_HEADS), F32), V((1, CH), F32),
            pltpu.SMEM((NB,), jnp.int32), V((1, BLOCK), jnp.int32), V((1, BLOCK), F32),
            V((BLOCK, CH), BF16),
            dma((15,)),
            V((SIDE, SIDE, 8, 128), F32),
            V((8, 8, 128), F32),
            V((2, NCH, SIDE, STATE, CW), BF16),
            V((2, SIDE, BLOCK, STATE), BF16),
            V((2, SIDE, STATE, BLOCK), BF16),
            V((2, NCH, SIDE, BLOCK, CW), BF16),
            V((2, NCH, SIDE, BLOCK, CW), BF16),
            V((2, NCH, SIDE, BLOCK, CW), BF16),
            V((2, NCH, SIDE, STATE, CW), BF16),
            V((2, NCH, SIDE, STATE, CW), BF16),
            V((4 + 2 * NCH, BLOCK, CW), F32),
            V((2, SIDE, SIDE, 8, HALF), F32),
            V((BLOCK, CH), F32),
            V((BLOCK, CH), F32),
            V((BLOCK, CH), F32),
            V((BLOCK, BLOCK), BF16),
            V((BLOCK, CH), F32),
            V((BLOCK, CH), F32),
            V((BLOCK, CH), F32),
            V((BLOCK, CH), F32),
            V((BLOCK, CH), F32),
            V((2, EARLY, SIDE, BLOCK, CW), BF16),
            V((2, EARLY, SIDE, BLOCK, CW), BF16),
            V((2, SIDE, 8, 128), F32),
            V((2, BLOCK, 128), F32),
            dma((2, EARLY, SIDE)), dma((2, EARLY, SIDE)),
            dma((2, EARLY, SIDE)), dma((2, EARLY, SIDE)),
            dma((2, SIDE)), dma((2, SIDE)),
            dma((2, SIDE)), dma((2, SIDE)), dma((8,)), dma((8,)),
            dma((2, NCH, SIDE)), dma((2, NCH, SIDE)),
            dma((2, SIDE)), dma((2, SIDE)),
            dma((2, NCH, SIDE)), dma((2, NCH, SIDE)),
            dma((2, NCH, SIDE)), dma((2, NCH, SIDE)),
            dma((2, NCH, SIDE)), dma((2, NCH, SIDE)),
        ],
        compiler_params=pltpu.CompilerParams(
            collective_id=0, has_side_effects=True, vmem_limit_bytes=40 * 2**20
        ),
    )(*(pltpu.with_memory_space_constraint(v, pltpu.HBM) for v in (
        prompt_x, prompt_b, prompt_dt, branch_x, branch_b, branch_c, branch_z, branch_dt,
        a_rate.reshape(1, -1), d_skip.reshape(1, -1), norm_gain.reshape(1, -1), branch_parent,
        group_ids.reshape(1, -1), returns.reshape(1, -1), out_grad,
    )))
    hbm = pl.BlockSpec(memory_space=pltpu.HBM)
    return pl.pallas_call(
        hand_over,
        out_shape=tuple(jax.ShapeDtypeStruct(r.shape, r.dtype) for r in results),
        in_specs=[vm] * 3,
        out_specs=(hbm,) * 3,
        scratch_shapes=[dma((3,))],
        compiler_params=pltpu.CompilerParams(vmem_limit_bytes=16 * 2**20),
    )(*results)


def solution(mesh):
    rows = P(("parts", "seq"), "head")
    steps = P("head", ("parts", "seq"))
    heads = P("head")
    tokens = P(("parts", "seq"))
    return jax.shard_map(
        local,
        mesh=mesh,
        in_specs=(
            rows, rows, steps, rows, rows, rows, rows, steps,
            heads, heads, heads, tokens, tokens, tokens, rows,
        ),
        out_specs=(rows, rows, rows),
        check_vma=False,
    )
```
